32 devices in a mesh: seq: 16 (over z, x, core), head: 2 (over y).
Axes of the slice: x: 2, y: 2, z: 4, core: 2. Of those that a mesh axis runs over, the one named last changes fastest.
Arguments:
- query: bfloat16 [2048, 32, 128], P(('seq', 'head')), may hold values from -40 to 40
- key: bfloat16 [2048, 32, 128], P(('seq', 'head')), may hold values from -40 to 40
- value: bfloat16 [2048, 32, 128], P(('seq', 'head')), may hold values from -6 to 6
- decay: float32 [2048, 32, 128], P(('seq', 'head')), may hold values from -1 to 0, as said below
- rate: float32 [2048, 32], P(('seq', 'head')), may hold values from 0.05 to 0.6
- carry_in: float32 [32, 128, 128], P('head'), may hold values from -3 to 3
- out_grad: bfloat16 [2048, 32, 128], P(('seq', 'head')), may hold values from -6 to 6
Outputs:
- output: bfloat16 [2048, 32, 128], P(('seq', 'head'))
- grad_query: bfloat16 [2048, 32, 128], P(('seq', 'head'))
- grad_key: bfloat16 [2048, 32, 128], P(('seq', 'head'))
- grad_value: bfloat16 [2048, 32, 128], P(('seq', 'head'))
- grad_decay: float32 [2048, 32, 128], P(('seq', 'head'))
- grad_rate: float32 [2048, 32], P(('seq', 'head'))
- states: float32 [16, 32, 128, 128], P('seq', 'head')
- state_grads: float32 [16, 32, 128, 128], P('seq', 'head')
The draws below stay inside these ranges and needn't reach their ends.
Inputs may be any that keep to these rules, and one draw needn't show every extreme that they name: `decay`: every entry is negative.
All inputs are finite; a program needn't handle non-finite values.
Results may differ from the reference program's by a relative error of at most 0.001.
Values may be sent and summed in bfloat16 or wider, within the bound.
No kernel may reach another device: no remote copies, remote signals or barrier semaphores. Data moves between devices by JAX's collectives and lax.ppermute only.
A program may use at most 192 MiB of HBM per device.

```python
import math
import jax
import jax.numpy as jnp
from jax import lax

H = 32
DK = 128
DV = 128
GROUP = 128
TOK_DEV = 128
BATCH_ELEMENTS = 2048


def scaled_rows(key, spread):
    first, second, third = jax.random.split(key, 3)
    base = jnp.clip(jax.random.normal(first, (BATCH_ELEMENTS, H, DK), jnp.float32), -4.0, 4.0)
    rows = jnp.exp(jax.random.uniform(second, (BATCH_ELEMENTS, H, 1), jnp.float32, 0.0, math.log(spread)))
    cols = jnp.exp(jax.random.uniform(third, (1, H, DK), jnp.float32, 0.0, math.log(spread)))
    return base * rows * cols / 10.0


def draw_query(key, part):
    key = jax.random.fold_in(key, 11)
    return scaled_rows(key, 10.0).astype(jnp.bfloat16)


def draw_key(key, part):
    key = jax.random.fold_in(key, 13)
    return scaled_rows(key, 10.0).astype(jnp.bfloat16)


def draw_decay(key, part):
    key = jax.random.fold_in(key, 17)
    keys = jax.random.split(key, 7)
    share = 0.5
    shortcut_route = jax.random.uniform(keys[0], (1, H, DK), jnp.float32) < share
    quick = jax.random.uniform(keys[1], (1, H, DK), jnp.float32, 0.046, 0.077)
    slow = jnp.exp(jax.random.uniform(keys[2], (1, H, DK), jnp.float32, math.log(2e-05), math.log(0.002)))
    speed = jnp.where(shortcut_route, quick, slow)
    shards = BATCH_ELEMENTS // TOK_DEV
    factor = jnp.exp(jax.random.uniform(keys[3], (shards, 1, H, DK), jnp.float32, math.log(0.5), math.log(2.0)))
    factor = jnp.broadcast_to(factor, (shards, TOK_DEV, H, DK)).reshape((BATCH_ELEMENTS, H, DK))
    rough = jax.random.uniform(keys[4], (BATCH_ELEMENTS, H, DK), jnp.float32, 0.5, 1.5)
    marked_locations = jax.random.randint(keys[5], (8,), 0, BATCH_ELEMENTS)
    element_group = jnp.any(jnp.arange(BATCH_ELEMENTS)[:, None] == marked_locations[None, :], axis=1)
    stack_height = jax.random.uniform(keys[6], (BATCH_ELEMENTS, H, DK), jnp.float32, math.log(0.5), math.log(0.8))
    additional_summands = jnp.where(element_group[:, None, None] & jnp.logical_not(shortcut_route), stack_height, 0.0)
    return (-speed * factor * rough + additional_summands).astype(jnp.float32)


def block_scale(rng, shape, cuts, low, top_value):
    factor_of = 1.0
    for axis_at, shards_of in cuts:
        heights = jax.random.uniform(jax.random.fold_in(jax.random.fold_in(rng, 6), axis_at), (shards_of,), jnp.float32, low / len(cuts), top_value / len(cuts))
        factor_of = factor_of * jnp.repeat(jnp.exp(heights), shape[axis_at] // shards_of).reshape((-1,) + (1,) * (len(shape) - 1 - axis_at))
    return factor_of


def gaussian(stream_key, dims, scale, bound, cuts=(), held_as=jnp.bfloat16):
    factor_of = block_scale(stream_key, dims, cuts, -0.22, 0.18) if cuts else 1.0
    array = jax.random.normal(stream_key, dims, jnp.float32) * scale * factor_of
    return jnp.minimum(jnp.maximum(array, -bound), bound).astype(held_as)


def setup_inputs(seed: int = 0) -> dict:
    key_of = jax.random.split(jax.random.key(seed), 8)
    return {
        "query": draw_query(jax.random.fold_in(key_of[7], 71), 0),
        "key": draw_key(jax.random.fold_in(key_of[7], 71), 0),
        "value": gaussian(key_of[2], (BATCH_ELEMENTS, H, DV), 1.0, 6.0, ((0, 32),)),
        "decay": draw_decay(jax.random.fold_in(key_of[7], 71), 0),
        "rate": jnp.clip(0.05 + 0.55 * jax.random.uniform(key_of[4], (BATCH_ELEMENTS, H), jnp.float32) ** block_scale(key_of[4], (BATCH_ELEMENTS, H), ((0, 32),), -0.2, 0.2), 0.05, 0.6),
        "carry_in": gaussian(key_of[5], (H, DK, DV), 0.5, 3.0, ((0, 2),), jnp.float32),
        "out_grad": gaussian(key_of[6], (BATCH_ELEMENTS, H, DV), 1.0, 6.0, ((0, 32),)),
    }


HIGH_ACCURACY = lax.Precision.HIGHEST

def unit(values):
    return values * lax.rsqrt(lax.optimization_barrier(jnp.sum(values * values, axis=-1, keepdims=True)) + 1e-06)

def group_step(state, block):
    query, key, value, decay, rate = block
    cum = jnp.cumsum(decay, axis=0)
    rise = jnp.exp(cum)
    kneg = key * jnp.exp(-cum)
    kpos = key * rise
    qpos = query * rise
    inner = jnp.einsum('thk,shk->hts', kpos, kneg, precision=HIGH_ACCURACY)
    cross = jnp.einsum('thk,shk->hts', qpos, kneg, precision=HIGH_ACCURACY)
    order = jnp.arange(decay.shape[0])
    below = order[:, None] > order[None, :]
    within = order[:, None] >= order[None, :]
    weight = jnp.transpose(rate)
    strict = jnp.where(below, inner, 0.0) * weight[:, :, None]
    known = jnp.einsum('thk,hkw->htw', kpos, state, precision=HIGH_ACCURACY)
    source = weight[:, :, None] * (jnp.transpose(value, (1, 0, 2)) - known)
    delta = jax.scipy.linalg.solve_triangular(strict, source, lower=True, unit_diagonal=True)
    out = jnp.einsum('thk,hkw->thw', qpos, state, precision=HIGH_ACCURACY)
    out = out + jnp.einsum('hts,hsw->thw', jnp.where(within, cross, 0.0), delta, precision=HIGH_ACCURACY)
    fade = jnp.exp(cum[-1][None] - cum)
    end = jnp.exp(cum[-1])[:, :, None] * state
    end = end + jnp.einsum('shk,hsw->hkw', key * fade, delta, precision=HIGH_ACCURACY)
    return (end, out)

def run_local(query, key, value, decay, rate, state):
    tok_count = query.shape[0]
    blocks = tok_count // GROUP

    def split(values):
        return values.reshape((blocks, GROUP) + values.shape[1:])
    end, outs = lax.scan(group_step, state, (split(query), split(key), split(value), split(decay), split(rate)))
    return (end, outs.reshape((tok_count, query.shape[1], value.shape[2])))

def reference(query, key, value, decay, rate, carry_in, out_grad):
    shards = BATCH_ELEMENTS // TOK_DEV

    def shape_up(values):
        return values.reshape((shards, TOK_DEV) + values.shape[1:])

    def forward(query_f, key_f, value_f, gate, beta, bump):
        pieces = (shape_up(unit(query_f)), shape_up(unit(key_f)), shape_up(value_f), shape_up(gate), shape_up(beta), bump)

        def shard(state, piece):
            entering = state + piece[5]
            end, out = run_local(piece[0], piece[1], piece[2], piece[3], piece[4], entering)
            return (end, (out, entering))
        final, (outs, entered) = lax.scan(shard, carry_in, pieces)
        return (outs.reshape((BATCH_ELEMENTS, H, DV)), entered)
    bump = jnp.zeros((shards, H, DK, DV), jnp.float32)
    full, pullback, states = jax.vjp(forward, query.astype(jnp.float32), key.astype(jnp.float32), value.astype(jnp.float32), decay, rate, bump, has_aux=True)
    grads = pullback(out_grad.astype(jnp.float32))
    return (full.astype(jnp.bfloat16), grads[0].astype(jnp.bfloat16), grads[1].astype(jnp.bfloat16), grads[2].astype(jnp.bfloat16), grads[3], grads[4], states, grads[5])
```

```python
import functools

import jax
import jax.numpy as jnp
from jax import lax
from jax.experimental import pallas as pl
from jax.experimental.pallas import tpu as pltpu
from jax.sharding import PartitionSpec as P

F32 = jnp.float32
BF16 = jnp.bfloat16
BLOCK = 128
CHUNKS = 1
VMEM_BYTES = 52 * 1024 * 1024
NN = (((1,), (0,)), ((), ()))
NT = (((1,), (1,)), ((), ()))


def halves(a):
    hi = a.astype(BF16)
    return hi, (a - hi.astype(F32)).astype(BF16)


def left(a):
    hi, lo = halves(a)
    return jnp.concatenate([hi, lo], axis=1)


def dot(a, b, dims=NN):
    return lax.dot_general(a, b, dims, preferred_element_type=F32)


def mm(lhs, b):
    hi, lo = halves(b)
    row = jnp.concatenate([hi, lo], axis=1)
    both = dot(lhs, jnp.concatenate([row, row], axis=0))
    n = b.shape[1]
    return both[:, :n] + both[:, n:]


def mm_t(lhs, b):
    hi, lo = halves(b)
    rows = jnp.concatenate([hi, lo], axis=0)
    both = dot(lhs, jnp.concatenate([rows, rows], axis=1), NT)
    n = b.shape[0]
    return both[:, :n] + both[:, n:]


def mm_exact(lhs, b):
    return dot(lhs, jnp.concatenate([b, b], axis=0))


def thirds(a):
    hi = a.astype(BF16)
    rest = a - hi.astype(F32)
    mid = rest.astype(BF16)
    return hi, mid, (rest - mid.astype(F32)).astype(BF16)


def ones_product(ones, a):
    n = a.shape[1]
    parts = dot(ones, jnp.concatenate(thirds(a), axis=1))
    return parts[:, :n] + parts[:, n : 2 * n] + parts[:, 2 * n :]


def rows_cols():
    shape = (BLOCK, BLOCK)
    return lax.broadcasted_iota(jnp.int32, shape, 0), lax.broadcasted_iota(jnp.int32, shape, 1)


def unit_rate(x):
    return lax.rsqrt(jnp.sum(x * x, axis=-1, keepdims=True) + 1e-06)


def params(kind=None):
    return pltpu.CompilerParams(vmem_limit_bytes=VMEM_BYTES, dimension_semantics=kind)


def struct(shape, dtype=F32):
    return jax.ShapeDtypeStruct(shape, dtype)


SMEM = pl.BlockSpec(memory_space=pltpu.SMEM)


def pack_kernel(d, sc, q, k, v, g, decay, rate, *outs_scratch):
    outs, scratch = outs_scratch[:-1], outs_scratch[-1]
    me = sc[0]
    nh, hg, hc, chunks, tl, heads = d["nh"], d["hg"], d["hc"], d["chunks"], d["tl"], d["heads"]
    for i, ref in enumerate((q, k, v, g, decay)):
        scratch[...] = jnp.swapaxes(ref[...].astype(F32), 0, 1)
        for j in range(chunks):
            for r in range(nh):
                bout, fout = outs[2 * (j * nh + r)], outs[2 * (j * nh + r) + 1]
                rows = scratch[pl.ds((me ^ r) * hg + j * hc, hc)]
                if i < 4:
                    bout[:, i] = rows.astype(BF16)
                else:
                    fout[:hc] = rows
    wide = jnp.concatenate([rate[...], jnp.zeros((tl, BLOCK - heads), F32)], axis=1)
    for j in range(chunks):
        for r in range(nh):
            outs[2 * (j * nh + r) + 1][hc] = wide


def pack(d, sc, q, k, v, g, decay, rate):
    shapes = []
    for _ in range(d["chunks"] * d["nh"]):
        shapes.append(struct((d["hc"], 4, d["tl"], BLOCK), BF16))
        shapes.append(struct((d["hc"] + 1, d["tl"], BLOCK)))
    vm = pl.BlockSpec(memory_space=pltpu.VMEM)
    return pl.pallas_call(
        functools.partial(pack_kernel, d),
        out_shape=shapes,
        in_specs=[SMEM] + [vm] * 6,
        out_specs=[vm] * len(shapes),
        scratch_shapes=[pltpu.VMEM((d["heads"], d["tl"], BLOCK), F32)],
        compiler_params=params(),
        name="pack",
    )(sc, q, k, v, g, decay, rate)


def local_kernel(d, j, sc, *refs):
    nh, hb, tl, hg, hc = d["nh"], d["hb"], d["tl"], d["hg"], d["hc"]
    bufs, rest = refs[: 2 * nh], refs[2 * nh :]
    keep, send, saved, raw, rates = rest
    half, step = pl.program_id(0), pl.program_id(1)
    me = sc[0]
    first = ((half ^ sc[1]) * (hc // 2)) + step * hb
    for r in range(nh):
        at = pl.multiple_of((me ^ r) * tl, tl)
        for u in range(hb):
            for i in range(4):
                raw[u, i, pl.ds(at, tl)] = bufs[2 * r][u, i].astype(F32)
            raw[u, 4, pl.ds(at, tl)] = bufs[2 * r + 1][first + u]
        rates[pl.ds(at, tl)] = bufs[2 * r + 1][hc]
    rows, cols = rows_cols()
    tri = jnp.where(rows >= cols, 1.0, 0.0).astype(BF16)
    apart = rows ^ cols
    table = rates[...]
    heads = range(hb)
    lower, cross, kpos, kend, qpos, fade, beta_rows = [], [], [], [], [], [], []
    for u in heads:
        q, k, decay = raw[u, 0], raw[u, 1], raw[u, 4]
        qn, kn = q * unit_rate(q), k * unit_rate(k)
        cum = ones_product(tri, decay)
        mid = 0.5 * cum[BLOCK - 1 :]
        grow = jnp.exp(cum - mid)
        shrink = jnp.exp(mid - cum)
        em = jnp.exp(mid)
        kc, kneg, qc = kn * grow, kn * shrink, qn * grow
        both = mm_t(left(jnp.concatenate([kc, qc], axis=0)), kneg)
        head = me * hg + j * hc + first + u
        beta = jnp.sum(jnp.where(cols == head, table, 0.0), axis=1, keepdims=True)
        lower.append(jnp.where(rows > cols, both[:BLOCK], 0.0) * beta)
        cross.append(jnp.where(rows >= cols, both[BLOCK:], 0.0))
        beta_rows.append(jnp.broadcast_to(beta, (BLOCK, BLOCK)).T)
        kpos.append(kc * em)
        qpos.append(qc * em)
        kend.append(kneg * em)
        fade.append(jnp.where(rows == cols, em * em, 0.0))
        saved[u, 6] = cum
    inverse = [jnp.where(rows == cols, 1.0, jnp.where(apart == 1, -lower[u], 0.0)) for u in heads]
    level = 1
    while (1 << level) < BLOCK:
        off = (apart >> level) == 1
        steps = [left(jnp.where(off, lower[u], 0.0)) for u in heads]
        mids = [mm(steps[u], inverse[u]) for u in heads]
        inverse = [inverse[u] - mm(left(inverse[u]), mids[u]) for u in heads]
        level += 1
    out = []
    for u in heads:
        v, g = raw[u, 2].astype(BF16), raw[u, 3].astype(BF16)
        solve = inverse[u] * beta_rows[u]
        wide = left(solve)
        p, uu = mm(wide, kpos[u]), mm_exact(wide, v)
        pair = left(jnp.concatenate([cross[u], kend[u].T], axis=0))
        by_p, by_u = mm(pair, p), mm(pair, uu)
        reach = qpos[u] - by_p[:BLOCK]
        seen = mm_exact(left(jnp.concatenate([reach.T, cross[u].T], axis=0)), g)
        back = left(solve.T)
        saved[u, 0] = p
        saved[u, 1] = uu
        saved[u, 2] = reach
        saved[u, 3] = by_u[:BLOCK]
        saved[u, 4] = mm(back, kend[u])
        saved[u, 5] = mm(back, seen[BLOCK:])
        out.append((fade[u] - by_p[BLOCK:], by_u[BLOCK:], seen[:BLOCK]))
    for side, ref in ((0, keep), (1, send)):

        @pl.when(half == side)
        def _(ref=ref):
            for u in heads:
                for i in range(3):
                    ref[u, i] = out[u][i]


def half_maps(last):
    keep = lambda h, i, *_: jnp.where(h == 0, i, last)
    send = lambda h, i, *_: jnp.where(h == 0, 0, i)
    return keep, send


def local_terms(d, j, sc, bufs):
    nh, hb, tl, hc = d["nh"], d["hb"], d["tl"], d["hc"]
    steps = hc // 2 // hb
    keep, send = half_maps(steps - 1)
    true = lambda h, i, sc: (h ^ sc[1]) * steps + i
    specs = []
    for _ in range(nh):
        specs.append(pl.BlockSpec((hb, 4, tl, BLOCK), lambda h, i, sc: (true(h, i, sc), 0, 0, 0)))
        specs.append(pl.BlockSpec((hc + 1, tl, BLOCK), lambda h, i, sc: (0, 0, 0)))
    triple = (hb, 3, BLOCK, BLOCK)
    return pl.pallas_call(
        functools.partial(local_kernel, d, j),
        out_shape=[
            struct((hc // 2, 3, BLOCK, BLOCK)),
            struct((hc // 2, 3, BLOCK, BLOCK)),
            struct((hc, 7, BLOCK, BLOCK)),
        ],
        grid_spec=pltpu.PrefetchScalarGridSpec(
            num_scalar_prefetch=1,
            grid=(2, steps),
            in_specs=specs,
            out_specs=[
                pl.BlockSpec(triple, lambda h, i, sc: (keep(h, i), 0, 0, 0)),
                pl.BlockSpec(triple, lambda h, i, sc: (send(h, i), 0, 0, 0)),
                pl.BlockSpec((hb, 7, BLOCK, BLOCK), lambda h, i, sc: (h * steps + i, 0, 0, 0)),
            ],
            scratch_shapes=[
                pltpu.VMEM((hb, 5, BLOCK, BLOCK), F32),
                pltpu.VMEM((BLOCK, BLOCK), F32),
            ],
        ),
        compiler_params=params(("arbitrary", "arbitrary")),
        name="local",
    )(sc, *bufs)


def forward_state(maps, h, state):
    return mm(left(maps[h, 0]), state) + maps[h, 1]


def backward_state(maps, h, grad):
    return mm(left(maps[h, 0].T), grad) + maps[h, 2]


def join_kernel(bit, side, n, sc, mine, other, keep, send):
    def run(a, b):
        for i in range(n):
            for ref, s in ((keep, sc[side]), (send, 1 - sc[side])):
                h = i if send is None else s * n + i
                later, early_t = left(b[h, 0]), left(a[h, 0].T)
                ref[i, 0] = mm(later, a[h, 0])
                ref[i, 1] = mm(later, a[h, 1]) + b[h, 1]
                ref[i, 2] = mm(early_t, b[h, 2]) + a[h, 2]

    @pl.when(sc[bit] == 0)
    def _():
        run(mine, other)

    @pl.when(sc[bit] == 1)
    def _():
        run(other, mine)


def vm_call(body, name, out_shape, *args):
    vm = pl.BlockSpec(memory_space=pltpu.VMEM)
    many = isinstance(out_shape, list)
    return pl.pallas_call(
        body,
        out_shape=out_shape,
        in_specs=[SMEM] + [vm] * (len(args) - 1),
        out_specs=[vm] * len(out_shape) if many else vm,
        compiler_params=params(),
        name=name,
    )(*args)


def join(sc, mine, other):
    n = mine.shape[0] // 2
    shape = (n, 3, BLOCK, BLOCK)
    body = functools.partial(join_kernel, 1, 2, n)
    return vm_call(body, "join", [struct(shape), struct(shape)], sc, mine, other)


def plane_kernel(j, hc, groups, sc, mine, other, carry, plane, up):
    n = hc // 4
    base = j * hc + sc[1] * (hc // 2) + sc[2] * n

    def run(a, b):
        for h in range(n):
            later, early_t = left(b[h, 0]), left(a[h, 0].T)
            plane[h, 0] = mm(later, a[h, 0])
            plane[h, 1] = mm(later, a[h, 1]) + b[h, 1]
            plane[h, 2] = mm(early_t, b[h, 2]) + a[h, 2]

    @pl.when(sc[2] == 0)
    def _():
        run(mine, other)

    @pl.when(sc[2] == 1)
    def _():
        run(other, mine)

    @pl.when(sc[3] == 0)
    def _():
        for h in range(n):
            up[h] = forward_state(plane, h, carry[base + h])

    @pl.when(sc[3] != 0)
    def _():
        for h in range(n):
            up[h] = plane[h, 1]


def middle_kernel(n, sc, plane, up, down, turn):
    @pl.when(sc[3] == 1)
    def _():
        for h in range(n):
            turn[h] = forward_state(plane, h, up[h])

    @pl.when(sc[3] == 2)
    def _():
        for h in range(n):
            turn[h] = backward_state(plane, h, down[h])

    @pl.when((sc[3] == 0) | (sc[3] == 3))
    def _():
        turn[...] = jnp.zeros_like(turn)


def spread_x(n, sc, state, grad, mine, other, keep, send):
    @pl.when(sc[2] == 0)
    def _():
        for h in range(n):
            keep[h, 0] = state[h]
            keep[h, 1] = backward_state(other, h, grad[h])
            send[h, 0] = forward_state(mine, h, state[h])
            send[h, 1] = grad[h]

    @pl.when(sc[2] == 1)
    def _():
        for h in range(n):
            keep[h, 0] = forward_state(other, h, state[h])
            keep[h, 1] = grad[h]
            send[h, 0] = state[h]
            send[h, 1] = backward_state(mine, h, grad[h])


def last_kernel(j, hc, sc, carry, up, down, map_in, near, far, mine, other, keep, send, state, grad):
    n = hc // 4
    base = j * hc + sc[1] * (hc // 2) + sc[2] * n

    @pl.when(sc[3] == 0)
    def _():
        for h in range(n):
            state[h] = carry[base + h]
            grad[h] = mm(left(map_in[h].T), far[h]) + down[h]

    @pl.when(sc[3] == 1)
    def _():
        state[...] = up[...]
        grad[...] = near[...]

    @pl.when(sc[3] == 2)
    def _():
        state[...] = near[...]
        grad[...] = down[...]

    @pl.when(sc[3] == 3)
    def _():
        for h in range(n):
            state[h] = mm(left(map_in[h]), far[h]) + up[h]
        grad[...] = jnp.zeros_like(grad)

    spread_x(n, sc, state, grad, mine, other, keep, send)


def hop_kernel(j, hc, groups, sc, plane, carry, up, down, after, before):
    n = hc // 4
    base = j * hc + sc[1] * (hc // 2) + sc[2] * n
    for h in range(n):
        entering = jnp.where(sc[3] == 0, carry[base + h], up[h])
        leaving = jnp.where(sc[3] == groups - 1, 0.0, down[h])
        after[h] = forward_state(plane, h, entering)
        before[h] = backward_state(plane, h, leaving)


def end_kernel(j, hc, groups, sc, carry, up, down, mine, other, keep, send, state, grad):
    n = hc // 4
    base = j * hc + sc[1] * (hc // 2) + sc[2] * n
    for h in range(n):
        state[h] = jnp.where(sc[3] == 0, carry[base + h], up[h])
        grad[h] = jnp.where(sc[3] == groups - 1, 0.0, down[h])
    spread_x(n, sc, state, grad, mine, other, keep, send)


def core_kernel(n, sc, own, came, mine, other, keep, send):
    def run(first):
        for half, source in ((sc[2], own), (1 - sc[2], came)):
            for i in range(n):
                h = half * n + i
                state, grad = source[i, 0], source[i, 1]
                if first:
                    keep[h, 0] = state
                    keep[h, 1] = backward_state(other, h, grad)
                    send[h, 0] = forward_state(mine, h, state)
                    send[h, 1] = grad
                else:
                    keep[h, 0] = forward_state(other, h, state)
                    keep[h, 1] = grad
                    send[h, 0] = state
                    send[h, 1] = backward_state(mine, h, grad)

    @pl.when(sc[1] == 0)
    def _():
        run(True)

    @pl.when(sc[1] == 1)
    def _():
        run(False)


def swap(array, n, stride):
    return lax.ppermute(array, "seq", [(i, i ^ stride) for i in range(n)])


def move(array, groups, pairs):
    return lax.ppermute(array, "seq", [(4 * a + k, 4 * b + k) for a, b in pairs for k in range(4)])


def scan_states(d, j, sc, keep, send, carry):
    n, hc, groups = d["n"], d["hc"], d["n"] // 4
    half, quarter = hc // 2, hc // 4
    came = swap(send, n, 1)
    keep_x, send_x = join(sc, keep, came)
    came_x = swap(send_x, n, 2)
    single = struct((quarter, BLOCK, BLOCK))
    plane, up = vm_call(
        functools.partial(plane_kernel, j, hc, groups),
        "plane",
        [struct((quarter, 3, BLOCK, BLOCK)), single],
        sc,
        keep_x,
        came_x,
        carry,
    )
    pair = struct((quarter, 2, BLOCK, BLOCK))
    scratch = [pltpu.VMEM((quarter, BLOCK, BLOCK), F32)] * 2
    vm = pl.BlockSpec(memory_space=pltpu.VMEM)

    def finish(body, *args):
        return pl.pallas_call(
            body,
            out_shape=[pair, pair],
            in_specs=[SMEM] + [vm] * (len(args) - 1),
            out_specs=[vm, vm],
            scratch_shapes=scratch,
            compiler_params=params(),
            name="spread",
        )(*args)

    if groups == 4:
        up_in = move(up, groups, [(0, 1), (2, 3)])
        down_in = move(plane[:, 2], groups, [(3, 2), (1, 0)])
        map_in = move(plane[:, 0], groups, [(2, 3), (1, 0)])
        turn = vm_call(
            functools.partial(middle_kernel, quarter), "middle", single, sc, plane, up_in, down_in
        )
        near = move(turn, groups, [(1, 2), (2, 1)])
        far = move(turn, groups, [(1, 3), (2, 0)])
        body = functools.partial(last_kernel, j, hc)
        own_x, give_x = finish(
            body, sc, carry, up_in, down_in, map_in, near, far, keep_x, came_x
        )
    else:
        up_in = jnp.zeros((quarter, BLOCK, BLOCK), F32)
        down_in = up_in
        upward = [(i, i + 1) for i in range(groups - 1)]
        downward = [(i + 1, i) for i in range(groups - 1)]
        body = functools.partial(hop_kernel, j, hc, groups)

        def hop(_, at):
            after, before = vm_call(body, "hop", [single, single], sc, plane, carry, *at)
            return move(after, groups, upward), move(before, groups, downward)

        up_in, down_in = lax.fori_loop(0, groups - 1, hop, (up_in, down_in))
        body = functools.partial(end_kernel, j, hc, groups)
        own_x, give_x = finish(body, sc, carry, up_in, down_in, keep_x, came_x)
    got_x = swap(give_x, n, 2)
    pair = struct((half, 2, BLOCK, BLOCK))
    body = functools.partial(core_kernel, quarter)
    own, give = vm_call(body, "core", [pair, pair], sc, own_x, got_x, keep, came)
    return own, swap(give, n, 1)


def final_kernel(d, j, sc, *refs):
    nh, hb, tl, hg, hc = d["nh"], d["hb"], d["tl"], d["hg"], d["hc"]
    bufs, refs = refs[: 2 * nh], refs[2 * nh :]
    keep, send, saved, own, came = refs[:5]
    outs = refs[5 : 5 + 2 * nh]
    states, state_grads, raw, rates, result, slopes = refs[5 + 2 * nh :]
    half, step = pl.program_id(0), pl.program_id(1)
    me = sc[0]
    first = ((half ^ sc[1]) * (hc // 2)) + step * hb
    for r in range(nh):
        at = pl.multiple_of((me ^ r) * tl, tl)
        for u in range(hb):
            for t, i in enumerate((0, 1, 3)):
                raw[u, t, pl.ds(at, tl)] = bufs[2 * r][u, i].astype(F32)
        rates[pl.ds(at, tl)] = bufs[2 * r + 1][0]
    rows, cols = rows_cols()
    upper = jnp.where(rows <= cols, 1.0, 0.0).astype(BF16)
    table = rates[...]
    heads = range(hb)

    @pl.when((half == 0) & (step == 0))
    def _():
        slopes[...] = jnp.zeros_like(slopes)

    mine = half == 0
    for u in heads:
        q, k, g = raw[u, 0], raw[u, 1], raw[u, 2]
        rq, rk = unit_rate(q), unit_rate(k)
        qn, kn = q * rq, k * rk
        cum = saved[u, 6]
        mid = 0.5 * cum[BLOCK - 1 :]
        grow, shrink, em = jnp.exp(cum - mid), jnp.exp(mid - cum), jnp.exp(mid)
        kc, kneg, qc = kn * grow, kn * shrink, qn * grow
        state = jnp.where(mine, own[u, 0], came[u, 0])
        grad = jnp.where(mine, own[u, 1], came[u, 1])
        transit = jnp.where(mine, keep[u, 0], send[u, 0])
        feed = jnp.where(mine, keep[u, 2], send[u, 2])
        known = mm(left(jnp.concatenate([saved[u, 0], saved[u, 2]], axis=0)), state)
        delta = saved[u, 1] - known[:BLOCK]
        result[u, 0] = saved[u, 3] + known[BLOCK:]
        pulled = mm(left(jnp.concatenate([saved[u, 4], transit.T], axis=0)), grad)
        dv = saved[u, 5] + pulled[:BLOCK]
        result[u, 3] = dv
        states[0, u] = state
        state_grads[0, u] = feed + pulled[BLOCK:]
        gd = left(jnp.concatenate([g, -dv], axis=0))
        weights = mm_t(gd, delta)
        cross = jnp.where(rows >= cols, weights[:BLOCK], 0.0)
        inner = jnp.where(rows > cols, weights[BLOCK:], 0.0)
        stacked = jnp.concatenate([cross, inner], axis=0)
        pos = mm(left(stacked), kneg) + em * mm_t(gd, state)
        dqc, dkc = pos[:BLOCK], pos[BLOCK:]
        tail = em * mm_t(left(delta), grad)
        dkneg = mm(left(cross.T), qc) + mm(left(inner.T), kc) + tail
        dqn = dqc * grow
        dkn = dkc * grow + dkneg * shrink
        result[u, 1] = rq * (dqn - qn * jnp.sum(qn * dqn, axis=1, keepdims=True))
        result[u, 2] = rk * (dkn - kn * jnp.sum(kn * dkn, axis=1, keepdims=True))
        dcum = qc * dqc + kc * dkc - kneg * dkneg
        scale = em * em
        mixed = jnp.sum((grad * state).T, axis=0, keepdims=True)
        end = jnp.sum(kneg * tail, axis=0, keepdims=True) + scale * mixed
        result[u, 4] = ones_product(upper, dcum) + end
        head = me * hg + j * hc + first + u
        beta = jnp.sum(jnp.where(cols == head, table, 0.0), axis=1, keepdims=True)
        slope = jnp.sum(dv * delta, axis=1, keepdims=True) / (beta * beta)
        slopes[...] += jnp.where(cols == head, slope, 0.0)
    for r in range(nh):
        at = pl.multiple_of((me ^ r) * tl, tl)
        for u in heads:
            for i in range(4):
                outs[2 * r][first + u, i] = result[u, i, pl.ds(at, tl)].astype(BF16)
            outs[2 * r + 1][first + u] = result[u, 4, pl.ds(at, tl)]
        outs[2 * r + 1][hc] = slopes[pl.ds(at, tl)]


def final_terms(d, j, sc, bufs, keep, send, saved, own, came):
    nh, hb, tl, hc = d["nh"], d["hb"], d["tl"], d["hc"]
    steps = hc // 2 // hb
    by_keep, by_send = half_maps(steps - 1)
    true = lambda h, i, sc: (h ^ sc[1]) * steps + i
    specs = []
    for _ in range(nh):
        specs.append(pl.BlockSpec((hb, 4, tl, BLOCK), lambda h, i, sc: (true(h, i, sc), 0, 0, 0)))
        specs.append(pl.BlockSpec((1, tl, BLOCK), lambda h, i, sc: (hc, 0, 0)))
    for width, which in ((3, by_keep), (3, by_send)):
        specs.append(
            pl.BlockSpec(
                (hb, width, BLOCK, BLOCK), lambda h, i, sc, which=which: (which(h, i), 0, 0, 0)
            )
        )
    specs.append(pl.BlockSpec((hb, 7, BLOCK, BLOCK), lambda h, i, sc: (h * steps + i, 0, 0, 0)))
    for which in (by_keep, by_send):
        specs.append(
            pl.BlockSpec(
                (hb, 2, BLOCK, BLOCK), lambda h, i, sc, which=which: (which(h, i), 0, 0, 0)
            )
        )
    out_shape, out_specs = [], []
    for _ in range(nh):
        out_shape.append(struct((hc, 4, tl, BLOCK), BF16))
        out_shape.append(struct((hc + 1, tl, BLOCK)))
        out_specs.append(pl.BlockSpec((hc, 4, tl, BLOCK), lambda h, i, sc: (0, 0, 0, 0)))
        out_specs.append(pl.BlockSpec((hc + 1, tl, BLOCK), lambda h, i, sc: (0, 0, 0)))
    for _ in range(2):
        out_shape.append(struct((1, hc, BLOCK, BLOCK)))
        out_specs.append(
            pl.BlockSpec((1, hb, BLOCK, BLOCK), lambda h, i, sc: (0, true(h, i, sc), 0, 0))
        )
    return pl.pallas_call(
        functools.partial(final_kernel, d, j),
        out_shape=out_shape,
        grid_spec=pltpu.PrefetchScalarGridSpec(
            num_scalar_prefetch=1,
            grid=(2, steps),
            in_specs=specs,
            out_specs=out_specs,
            scratch_shapes=[
                pltpu.VMEM((hb, 3, BLOCK, BLOCK), F32),
                pltpu.VMEM((BLOCK, BLOCK), F32),
                pltpu.VMEM((hb, 5, BLOCK, BLOCK), F32),
                pltpu.VMEM((BLOCK, BLOCK), F32),
            ],
        ),
        compiler_params=params(("arbitrary", "arbitrary")),
        name="final",
    )(sc, *bufs, keep, send, saved, own, came)


def unpack_kernel(d, sc, *refs):
    nh, hg, hc, chunks, tl, heads = d["nh"], d["hg"], d["hc"], d["chunks"], d["tl"], d["heads"]
    ins, outs, scratch = refs[: 2 * chunks * nh], refs[2 * chunks * nh : -1], refs[-1]
    me = sc[0]
    slopes = jnp.zeros((tl, BLOCK), F32)
    for i in range(5):
        for j in range(chunks):
            for r in range(nh):
                bin_, fin = ins[2 * (j * nh + r)], ins[2 * (j * nh + r) + 1]
                rows = bin_[:, i].astype(F32) if i < 4 else fin[:hc]
                scratch[pl.ds((me ^ r) * hg + j * hc, hc)] = rows
                if i == 4:
                    slopes += fin[hc]
        outs[i][...] = jnp.swapaxes(scratch[...], 0, 1).astype(outs[i].dtype)
    outs[5][...] = slopes[:, :heads]


def unpack(d, sc, bufs):
    tl, heads = d["tl"], d["heads"]
    full = (tl, heads, BLOCK)
    shapes = [struct(full, BF16)] * 4 + [struct(full), struct((tl, heads))]
    vm = pl.BlockSpec(memory_space=pltpu.VMEM)
    return pl.pallas_call(
        functools.partial(unpack_kernel, d),
        out_shape=shapes,
        in_specs=[SMEM] + [vm] * len(bufs),
        out_specs=[vm] * 6,
        scratch_shapes=[pltpu.VMEM((heads, tl, BLOCK), F32)],
        compiler_params=params(),
        name="unpack",
    )(sc, *bufs)


def exchange(d, bufs):
    nh = d["nh"]
    return [
        buf if r == 0 else lax.ppermute(buf, "head", [(i, i ^ r) for i in range(nh)])
        for r in range(nh)
        for buf in bufs[2 * r : 2 * r + 2]
    ]


def per_device(d, query, key, value, decay, rate, carry_in, out_grad):
    place = lax.axis_index("seq")
    sc = jnp.stack(
        [lax.axis_index("head"), place & 1, (place >> 1) & 1, place >> 2]
    ).astype(jnp.int32)
    nh, chunks = d["nh"], d["chunks"]
    packed = pack(d, sc, query, key, value, out_grad, decay, rate)
    back, states, state_grads = [], [], []
    for j in range(chunks):
        bufs = exchange(d, packed[2 * nh * j : 2 * nh * (j + 1)])
        keep, send, saved = local_terms(d, j, sc, bufs)
        own, came = scan_states(d, j, sc, keep, send, carry_in)
        *out, state, state_grad = final_terms(d, j, sc, bufs, keep, send, saved, own, came)
        back += exchange(d, out)
        states.append(state)
        state_grads.append(state_grad)
    outs = unpack(d, sc, back)
    if chunks > 1:
        return (*outs, jnp.concatenate(states, axis=1), jnp.concatenate(state_grads, axis=1))
    return (*outs, states[0], state_grads[0])


def solution(mesh):
    tokens = P(("seq", "head"), None, None)
    per_block = P("seq", "head", None, None)
    table = P(("seq", "head"), None)

    def run(query, key, value, decay, rate, carry_in, out_grad):
        n, nh = mesh.shape["seq"], mesh.shape["head"]
        heads = query.shape[1]
        hg = heads // nh
        chunks = CHUNKS if hg % (4 * CHUNKS) == 0 else 1
        hc = hg // chunks
        d = {
            "n": n,
            "nh": nh,
            "heads": heads,
            "hg": hg,
            "chunks": chunks,
            "hc": hc,
            "hb": min(4, hc // 2),
            "tl": query.shape[0] // (n * nh),
        }
        return jax.shard_map(
            functools.partial(per_device, d),
            mesh=mesh,
            in_specs=(tokens,) * 4 + (table, P("head", None, None), tokens),
            out_specs=(tokens,) * 5 + (table, per_block, per_block),
            check_vma=False,
        )(query, key, value, decay, rate, carry_in, out_grad)

    return run
```

```python
import functools

import jax
import jax.numpy as jnp
from jax import lax
from jax.experimental import pallas as pl
from jax.experimental.pallas import tpu as pltpu
from jax.sharding import PartitionSpec as P

F32 = jnp.float32
BF16 = jnp.bfloat16
BLOCK = 128
CHUNKS = 2
ROWS = 16
PACK_BYTES = 52 * 1024 * 1024
HB = 8
VMEM_BYTES = 26 * 1024 * 1024
NN = (((1,), (0,)), ((), ()))
NT = (((1,), (1,)), ((), ()))


def halves(a):
    hi = a.astype(BF16)
    return hi, (a - hi.astype(F32)).astype(BF16)


def left(a):
    hi, lo = halves(a)
    return jnp.concatenate([hi, lo], axis=1)


def dot(a, b, dims=NN):
    return lax.dot_general(a, b, dims, preferred_element_type=F32)


def mm(lhs, b):
    hi, lo = halves(b)
    row = jnp.concatenate([hi, lo], axis=1)
    both = dot(lhs, jnp.concatenate([row, row], axis=0))
    n = b.shape[1]
    return both[:, :n] + both[:, n:]


def mm_t(lhs, b):
    hi, lo = halves(b)
    rows = jnp.concatenate([hi, lo], axis=0)
    both = dot(lhs, jnp.concatenate([rows, rows], axis=1), NT)
    n = b.shape[0]
    return both[:, :n] + both[:, n:]


def mm_exact(lhs, b):
    return dot(lhs, jnp.concatenate([b, b], axis=0))


def thirds(a):
    hi = a.astype(BF16)
    rest = a - hi.astype(F32)
    mid = rest.astype(BF16)
    return hi, mid, (rest - mid.astype(F32)).astype(BF16)


def ones_product(ones, a):
    n = a.shape[1]
    parts = dot(ones, jnp.concatenate(thirds(a), axis=1))
    return parts[:, :n] + parts[:, n : 2 * n] + parts[:, 2 * n :]


def rows_cols():
    shape = (BLOCK, BLOCK)
    return lax.broadcasted_iota(jnp.int32, shape, 0), lax.broadcasted_iota(jnp.int32, shape, 1)


def unit_rate(x):
    return lax.rsqrt(jnp.sum(x * x, axis=-1, keepdims=True) + 1e-06)


def params(kind=None):
    return pltpu.CompilerParams(vmem_limit_bytes=VMEM_BYTES, dimension_semantics=kind)


def struct(shape, dtype=F32):
    return jax.ShapeDtypeStruct(shape, dtype)


SMEM = pl.BlockSpec(memory_space=pltpu.SMEM)


def cost(micros):
    return pl.CostEstimate(flops=int(micros * 1e10), bytes_accessed=0, transcendentals=0)


def pack_kernel(d, sc, q, k, v, g, decay, rate, *outs_scratch):
    outs, scratch = outs_scratch[:-1], outs_scratch[-1]
    me = sc[0]
    nh, hg, hc, chunks, heads = d["nh"], d["hg"], d["hc"], d["chunks"], d["heads"]
    for i, ref in enumerate((q, k, v, g, decay)):
        scratch[...] = jnp.swapaxes(ref[...].astype(F32), 0, 1)
        for j in range(chunks):
            for r in range(nh):
                bout, fout = outs[2 * (j * nh + r)], outs[2 * (j * nh + r) + 1]
                rows = scratch[pl.ds((me ^ r) * hg + j * hc, hc)]
                if i < 4:
                    bout[:, i] = rows.astype(BF16)
                else:
                    fout[:hc] = rows
    wide = jnp.concatenate([rate[...], jnp.zeros((ROWS, BLOCK - heads), F32)], axis=1)
    for j in range(chunks):
        for r in range(nh):
            outs[2 * (j * nh + r) + 1][hc] = wide


def pack(d, sc, q, k, v, g, decay, rate):
    hc, tl, heads = d["hc"], d["tl"], d["heads"]
    shapes, specs = [], []
    for _ in range(d["chunks"] * d["nh"]):
        shapes.append(struct((hc, 4, tl, BLOCK), BF16))
        shapes.append(struct((hc + 1, tl, BLOCK)))
        specs.append(pl.BlockSpec((hc, 4, ROWS, BLOCK), lambda i: (0, 0, i, 0)))
        specs.append(pl.BlockSpec((hc + 1, ROWS, BLOCK), lambda i: (0, i, 0)))
    block = pl.BlockSpec((ROWS, heads, BLOCK), lambda i: (i, 0, 0))
    return pl.pallas_call(
        functools.partial(pack_kernel, d),
        out_shape=shapes,
        grid=(tl // ROWS,),
        in_specs=[SMEM] + [block] * 5 + [pl.BlockSpec((ROWS, heads), lambda i: (i, 0))],
        out_specs=specs,
        scratch_shapes=[pltpu.VMEM((heads, ROWS, BLOCK), F32)],
        compiler_params=pltpu.CompilerParams(
            vmem_limit_bytes=PACK_BYTES, dimension_semantics=("arbitrary",)
        ),
        cost_estimate=cost(4),
        name="pack",
    )(sc, q, k, v, g, decay, rate)


def order(d, sc, step):
    part = d["hb"] // 2
    places = []
    for u in range(d["hb"]):
        half, i = u // part, step * part + u % part
        places.append((half, u % part, (half ^ sc[1]) * (d["hc"] // 2) + i))
    return places


def gather_rows(d, me, bufs, places, halves_ref, wide_ref, table, last):
    tl = d["tl"]
    for r in range(d["nh"]):
        at = pl.multiple_of((me ^ r) * tl, tl)
        for u, (_, _, h) in enumerate(places):
            for i in range(4):
                halves_ref[u, i, pl.ds(at, tl)] = bufs[2 * r][h, i]
            if wide_ref is not None:
                wide_ref[u, pl.ds(at, tl)] = bufs[2 * r + 1][h]
        table[pl.ds(at, tl)] = bufs[2 * r + 1][last]


def spread_rate(table, head):
    rows = lax.broadcasted_iota(jnp.int32, (3 * BLOCK, BLOCK), 0)
    pick = jnp.where((rows & (BLOCK - 1)) == head, 1.0, 0.0).astype(BF16)
    return dot(table, pick)


def lane_sums(x, ones):
    return mm_exact(left(x), ones)


def local_kernel(d, j, sc, *refs):
    nh, hb, hg, hc = d["nh"], d["hb"], d["hg"], d["hc"]
    bufs = refs[: 2 * nh]
    keep, send, (saved, thin, wide_rows, rates) = refs[-8], refs[-7:-4], refs[-4:]
    me = sc[0]
    places = order(d, sc, pl.program_id(0))
    gather_rows(d, me, bufs, places, thin, wide_rows, rates, hc)
    rows, cols = rows_cols()
    tri = jnp.where(rows >= cols, 1.0, 0.0).astype(BF16)
    ones = jnp.ones((BLOCK, BLOCK), BF16)
    apart = rows ^ cols
    table = jnp.concatenate(thirds(rates[...]), axis=1)
    heads = range(hb)
    lower, cross, crosst, kpos, kend, qpos, fade, beta = [], [], [], [], [], [], [], []
    for u in heads:
        half, i, h = places[u]
        q, k, decay = thin[u, 0].astype(F32), thin[u, 1].astype(F32), wide_rows[u]
        qn = q * lax.rsqrt(lane_sums(q * q, ones) + 1e-06)
        kn = k * lax.rsqrt(lane_sums(k * k, ones) + 1e-06)
        cum = ones_product(tri, decay)
        mid = 0.5 * cum[BLOCK - 1 :]
        grow = jnp.exp(cum - mid)
        shrink = jnp.exp(mid - cum)
        em = jnp.exp(mid)
        kc, kneg, qc = kn * grow, kn * shrink, qn * grow
        both = mm_t(left(jnp.concatenate([kc, qc], axis=0)), kneg)
        beta.append(spread_rate(table, me * hg + j * hc + h))
        lower.append(jnp.where(rows > cols, both[:BLOCK], 0.0) * beta[u])
        cross.append(jnp.where(rows >= cols, both[BLOCK:], 0.0))
        crosst.append(jnp.where(rows <= cols, mm_t(left(kneg), qc), 0.0))
        kpos.append(kc * em)
        qpos.append(qc * em)
        kend.append(kneg * em)
        fade.append(jnp.where(rows == cols, em * em, 0.0))
        saved[half, i, 6] = cum
    inverse = [jnp.where(rows == cols, 1.0, jnp.where(apart == 1, -lower[u], 0.0)) for u in heads]
    level = 1
    while (1 << level) < BLOCK:
        off = (apart >> level) == 1
        steps = [left(jnp.where(off, lower[u], 0.0)) for u in heads]
        mids = [mm(steps[u], inverse[u]) for u in heads]
        inverse = [inverse[u] - mm(left(inverse[u]), mids[u]) for u in heads]
        level += 1
    for u in heads:
        half, i, _ = places[u]
        v, g = thin[u, 2].astype(F32), thin[u, 3]
        scaled = jnp.concatenate([beta[u] * kpos[u], beta[u] * v], axis=1)
        solved = mm(left(inverse[u]), scaled)
        by = mm(left(jnp.concatenate([cross[u], kend[u].T], axis=0)), solved)
        reach = qpos[u] - by[:BLOCK, :BLOCK]
        hi, lo = halves(reach)
        feed = dot(g.T, jnp.concatenate([hi, lo], axis=1))
        own = (fade[u] - by[BLOCK:, :BLOCK], by[BLOCK:, BLOCK:], feed[:, :BLOCK] + feed[:, BLOCK:])
        for t in range(3):
            if half:
                send[t][i] = own[t]
            else:
                keep[i, t] = own[t]
        saved[half, i, 0] = solved[:, :BLOCK]
        saved[half, i, 1] = solved[:, BLOCK:]
        saved[half, i, 2] = reach
        saved[half, i, 3] = by[:BLOCK, BLOCK:]
        seen = mm_exact(left(crosst[u]), g)
        back = mm(left(inverse[u].T), jnp.concatenate([kend[u], seen], axis=1))
        saved[half, i, 4] = beta[u] * back[:, :BLOCK]
        saved[half, i, 5] = beta[u] * back[:, BLOCK:]


ANY = pl.BlockSpec(memory_space=pl.ANY)


def local_terms(d, j, sc, bufs, after):
    nh, hb, tl, hc = d["nh"], d["hb"], d["tl"], d["hc"]
    part = hb // 2
    specs = []
    for _ in range(nh):
        specs.append(pl.BlockSpec((hc, 4, tl, BLOCK), lambda i, sc: (0, 0, 0, 0)))
        specs.append(pl.BlockSpec((hc + 1, tl, BLOCK), lambda i, sc: (0, 0, 0)))
    triple = pl.BlockSpec((part, 3, BLOCK, BLOCK), lambda i, sc: (i, 0, 0, 0))
    return pl.pallas_call(
        functools.partial(local_kernel, d, j),
        out_shape=[
            struct((hc // 2, 3, BLOCK, BLOCK)),
            *[struct((hc // 2, BLOCK, BLOCK))] * 3,
            struct((2, hc // 2, 7, BLOCK, BLOCK)),
        ],
        grid_spec=pltpu.PrefetchScalarGridSpec(
            num_scalar_prefetch=1,
            grid=(hc // hb,),
            in_specs=specs + [ANY] * len(after),
            out_specs=[
                triple,
                *[pl.BlockSpec((part, BLOCK, BLOCK), lambda i, sc: (i, 0, 0))] * 3,
                pl.BlockSpec((2, part, 7, BLOCK, BLOCK), lambda i, sc: (0, i, 0, 0, 0)),
            ],
            scratch_shapes=[
                pltpu.VMEM((hb, 4, BLOCK, BLOCK), BF16),
                pltpu.VMEM((hb, BLOCK, BLOCK), F32),
                pltpu.VMEM((BLOCK, BLOCK), F32),
            ],
        ),
        compiler_params=params(("arbitrary",)),
        cost_estimate=cost(10),
        name="local",
    )(sc, *bufs, *after)


def term(maps, h, i):
    return maps[i][h] if isinstance(maps, tuple) else maps[h, i]


def forward_state(maps, h, state):
    return mm(left(term(maps, h, 0)), state) + term(maps, h, 1)


def backward_state(maps, h, grad):
    return mm(left(grad), term(maps, h, 0)) + term(maps, h, 2)


def join_maps(a, b, h, ref, i):
    by = mm(left(jnp.concatenate([term(b, h, 0), term(b, h, 2)], axis=0)), term(a, h, 0))
    ref[i, 0] = by[:BLOCK]
    ref[i, 1] = mm(left(term(b, h, 0)), term(a, h, 1)) + term(b, h, 1)
    ref[i, 2] = by[BLOCK:] + term(a, h, 2)


def join_kernel(n, sc, mine, *refs):
    other, (keep, send) = tuple(refs[:3]), refs[3:]

    def run(a, b):
        for i in range(n):
            for ref, s in ((keep, sc[2]), (send, 1 - sc[2])):
                join_maps(a, b, s * n + i, ref, i)

    @pl.when(sc[1] == 0)
    def _():
        run(mine, other)

    @pl.when(sc[1] == 1)
    def _():
        run(other, mine)


def vm_call(body, name, out_shape, *args, scratch=()):
    vm = pl.BlockSpec(memory_space=pltpu.VMEM)
    many = isinstance(out_shape, list)
    reads, waits = len(args) - 1, len(args[-1])

    def skip(*refs):
        body(*refs[:reads], *refs[reads + waits :])

    return pl.pallas_call(
        skip,
        out_shape=out_shape,
        in_specs=[SMEM] + [vm] * (len(args) - 2) + [ANY] * len(args[-1]),
        out_specs=[vm] * len(out_shape) if many else vm,
        scratch_shapes=list(scratch),
        compiler_params=params(),
        cost_estimate=cost(1),
        name=name,
    )(*args[:-1], *args[-1])


def carry_base(j, hc, sc):
    return j * hc + sc[1] * (hc // 2) + sc[2] * (hc // 4)


def plane_kernel(j, hc, sc, mine, other, carry, plane, pay):
    n = hc // 4
    base = carry_base(j, hc, sc)

    def run(a, b):
        for h in range(n):
            join_maps(a, b, h, plane, h)

    @pl.when(sc[2] == 0)
    def _():
        run(mine, other)

    @pl.when(sc[2] == 1)
    def _():
        run(other, mine)

    pay[:, 1] = plane[:, 0]

    @pl.when(sc[3] == 0)
    def _():
        for h in range(n):
            pay[h, 0] = forward_state(plane, h, carry[base + h])

    @pl.when((sc[3] != 0) & (sc[3] & 1 == 0))
    def _():
        pay[:, 0] = plane[:, 1]

    @pl.when(sc[3] & 1 == 1)
    def _():
        pay[:, 0] = plane[:, 2]


def middle_kernel(n, sc, plane, got, turn):
    @pl.when(sc[3] == 1)
    def _():
        for h in range(n):
            turn[h] = forward_state(plane, h, got[h, 0])

    @pl.when(sc[3] == 2)
    def _():
        for h in range(n):
            turn[h] = backward_state(plane, h, got[h, 0])

    @pl.when((sc[3] == 0) | (sc[3] == 3))
    def _():
        turn[...] = jnp.zeros_like(turn)


def spread_x(n, sc, state, grad, mine, other, keep, send):
    @pl.when(sc[2] == 0)
    def _():
        for h in range(n):
            keep[h, 0] = state[h]
            keep[h, 1] = backward_state(other, h, grad[h])
            send[h, 0] = forward_state(mine, h, state[h])
            send[h, 1] = grad[h]

    @pl.when(sc[2] == 1)
    def _():
        for h in range(n):
            keep[h, 0] = forward_state(other, h, state[h])
            keep[h, 1] = grad[h]
            send[h, 0] = state[h]
            send[h, 1] = backward_state(mine, h, grad[h])


def last_kernel(j, hc, sc, carry, got, near, far, mine, other, keep, send, state, grad):
    n = hc // 4
    base = carry_base(j, hc, sc)

    @pl.when(sc[3] == 0)
    def _():
        for h in range(n):
            state[h] = carry[base + h]
            grad[h] = mm(left(far[h]), got[h, 1]) + got[h, 0]

    @pl.when(sc[3] == 1)
    def _():
        state[...] = got[:, 0]
        grad[...] = near[...]

    @pl.when(sc[3] == 2)
    def _():
        state[...] = near[...]
        grad[...] = got[:, 0]

    @pl.when(sc[3] == 3)
    def _():
        for h in range(n):
            state[h] = mm(left(got[h, 1]), far[h]) + got[h, 0]
        grad[...] = jnp.zeros_like(grad)

    spread_x(n, sc, state, grad, mine, other, keep, send)


def hop_kernel(j, hc, groups, sc, plane, carry, up, down, ahead, behind):
    base = carry_base(j, hc, sc)
    for h in range(hc // 4):
        entering = jnp.where(sc[3] == 0, carry[base + h], up[h])
        leaving = jnp.where(sc[3] == groups - 1, 0.0, down[h])
        ahead[h] = forward_state(plane, h, entering)
        behind[h] = backward_state(plane, h, leaving)


def end_kernel(j, hc, groups, sc, carry, up, down, mine, other, keep, send, state, grad):
    n = hc // 4
    base = carry_base(j, hc, sc)
    for h in range(n):
        state[h] = jnp.where(sc[3] == 0, carry[base + h], up[h])
        grad[h] = jnp.where(sc[3] == groups - 1, 0.0, down[h])
    spread_x(n, sc, state, grad, mine, other, keep, send)


def core_kernel(n, sc, own, came, mine, *refs):
    other, (keep, send) = tuple(refs[:3]), refs[3:]

    def run(first):
        for half, source in ((sc[2], own), (1 - sc[2], came)):
            for i in range(n):
                h = half * n + i
                state, grad = source[i, 0], source[i, 1]
                if first:
                    keep[h, 0] = state
                    keep[h, 1] = backward_state(other, h, grad)
                    send[h, 0] = forward_state(mine, h, state)
                    send[h, 1] = grad
                else:
                    keep[h, 0] = forward_state(other, h, state)
                    keep[h, 1] = grad
                    send[h, 0] = state
                    send[h, 1] = backward_state(mine, h, grad)

    @pl.when(sc[1] == 0)
    def _():
        run(True)

    @pl.when(sc[1] == 1)
    def _():
        run(False)


def swap(array, n, stride):
    return lax.ppermute(array, "seq", [(i, i ^ stride) for i in range(n)])


def move(array, pairs):
    return lax.ppermute(array, "seq", [(4 * a + k, 4 * b + k) for a, b in pairs for k in range(4)])


def chunk_steps(d, j, sc, bufs, carry):
    n, hc, groups = d["n"], d["hc"], d["n"] // 4
    half, quarter = hc // 2, hc // 4
    single = struct((quarter, BLOCK, BLOCK))
    pair = struct((quarter, 2, BLOCK, BLOCK))
    pair_c = struct((half, 2, BLOCK, BLOCK))
    triple = struct((quarter, 3, BLOCK, BLOCK))
    scratch = [pltpu.VMEM((quarter, BLOCK, BLOCK), F32)] * 2
    after = yield
    keep, *send, saved = local_terms(d, j, sc, bufs, after)
    after = yield keep
    came = [swap(part, n, 1) for part in send]
    body = functools.partial(join_kernel, quarter)
    keep_x, send_x = vm_call(body, "join", [triple, triple], sc, keep, *came, after)
    after = yield send_x
    came_x = swap(send_x, n, 2)
    body = functools.partial(plane_kernel, j, hc)
    plane, pay = vm_call(body, "plane", [triple, pair], sc, keep_x, came_x, carry, after)
    after = yield pay
    if groups == 4:
        got = move(pay, [(0, 1), (1, 0), (2, 3), (3, 2)])
        body = functools.partial(middle_kernel, quarter)
        turn = vm_call(body, "middle", single, sc, plane, got, after)
        after = yield turn
        near = move(turn, [(1, 2), (2, 1)])
        far = move(turn, [(1, 3), (2, 0)])
        body = functools.partial(last_kernel, j, hc)
        args = (sc, carry, got, near, far, keep_x, came_x, after)
        own_x, give_x = vm_call(body, "spread", [pair, pair], *args, scratch=scratch)
    else:
        up_in = jnp.zeros((quarter, BLOCK, BLOCK), F32)
        down_in = up_in
        upward = [(i, i + 1) for i in range(groups - 1)]
        downward = [(i + 1, i) for i in range(groups - 1)]
        body = functools.partial(hop_kernel, j, hc, groups)

        def hop(_, at):
            ahead, behind = vm_call(body, "hop", [single, single], sc, plane, carry, *at, [])
            return move(ahead, upward), move(behind, downward)

        up_in, down_in = lax.fori_loop(0, groups - 1, hop, (up_in, down_in))
        after = yield up_in
        body = functools.partial(end_kernel, j, hc, groups)
        args = (sc, carry, up_in, down_in, keep_x, came_x, after)
        own_x, give_x = vm_call(body, "spread", [pair, pair], *args, scratch=scratch)
    after = yield give_x
    got_x = swap(give_x, n, 2)
    body = functools.partial(core_kernel, quarter)
    own, give = vm_call(body, "core", [pair_c, pair_c], sc, own_x, got_x, keep, *came, after)
    after = yield give
    arrived = swap(give, n, 1)
    outs = final_terms(d, j, sc, bufs, keep, send, saved, own, arrived, after)
    yield outs


def final_kernel(d, j, sc, *refs):
    nh, hb, tl, hg, hc = d["nh"], d["hb"], d["tl"], d["hg"], d["hc"]
    bufs, refs = refs[: 2 * nh], refs[2 * nh :]
    keep, send, (saved, own, came) = refs[0], refs[1:3], refs[3:6]
    outs = refs[-6 - 2 * nh : -6]
    states, state_grads, thin, rates, result, slopes = refs[-6:]
    step = pl.program_id(0)
    me = sc[0]
    places = order(d, sc, step)
    gather_rows(d, me, bufs, places, thin, None, rates, 0)
    rows, cols = rows_cols()
    upper = jnp.where(rows <= cols, 1.0, 0.0).astype(BF16)
    ones = jnp.ones((BLOCK, BLOCK), BF16)
    table = jnp.concatenate(thirds(rates[...]), axis=1)
    heads = range(hb)

    @pl.when(step == 0)
    def _():
        slopes[...] = jnp.zeros_like(slopes)

    for u in heads:
        half, i, h = places[u]
        ends = came if half else own
        transit = send[0][i] if half else keep[i, 0]
        feed = send[1][i] if half else keep[i, 2]
        q, k, g = thin[u, 0].astype(F32), thin[u, 1].astype(F32), thin[u, 3].astype(F32)
        rq = lax.rsqrt(lane_sums(q * q, ones) + 1e-06)
        rk = lax.rsqrt(lane_sums(k * k, ones) + 1e-06)
        qn, kn = q * rq, k * rk
        cum = saved[half, i, 6]
        mid = 0.5 * cum[BLOCK - 1 :]
        grow, shrink, em = jnp.exp(cum - mid), jnp.exp(mid - cum), jnp.exp(mid)
        kc, kneg, qc = kn * grow, kn * shrink, qn * grow
        state, grad = ends[i, 0], ends[i, 1]
        known = mm(left(jnp.concatenate([saved[half, i, 0], saved[half, i, 2]], axis=0)), state)
        delta = saved[half, i, 1] - known[:BLOCK]
        result[u, 0] = saved[half, i, 3] + known[BLOCK:]
        dv = saved[half, i, 5] + mm_t(left(saved[half, i, 4]), grad)
        result[u, 3] = dv
        states[0, h] = state
        wide_d, wide_s = left(delta), left(state)
        by_grad = mm(jnp.concatenate([wide_d, wide_s], axis=0), grad)
        tail = em * by_grad[:BLOCK]
        mixed = jnp.sum(jnp.where(rows == cols, by_grad[BLOCK:], 0.0), axis=0, keepdims=True)
        state_grads[0, h] = (feed + mm(left(grad), transit)).T
        both = jnp.concatenate([g, -dv], axis=0)
        gd = left(both)
        weights = mm_t(gd, delta)
        flipped = mm_t(wide_d, both)
        cross = jnp.where(rows >= cols, weights[:BLOCK], 0.0)
        inner = jnp.where(rows > cols, weights[BLOCK:], 0.0)
        crosst = jnp.where(rows <= cols, flipped[:, :BLOCK], 0.0)
        innert = jnp.where(rows < cols, flipped[:, BLOCK:], 0.0)
        pos = mm(left(jnp.concatenate([cross, inner], axis=0)), kneg) + em * mm_t(gd, state)
        dqc, dkc = pos[:BLOCK], pos[BLOCK:]
        dkneg = tail + mm(
            left(jnp.concatenate([crosst, innert], axis=1)), jnp.concatenate([qc, kc], axis=0)
        )
        dqn = dqc * grow
        dkn = dkc * grow + dkneg * shrink
        result[u, 1] = rq * (dqn - qn * lane_sums(qn * dqn, ones))
        result[u, 2] = rk * (dkn - kn * lane_sums(kn * dkn, ones))
        dcum = qc * dqc + kc * dkc - kneg * dkneg
        end = jnp.sum(kneg * tail, axis=0, keepdims=True) + em * em * mixed
        result[u, 4] = ones_product(upper, dcum) + end
        head = me * hg + j * hc + h
        beta = spread_rate(table, head)
        slope = lane_sums(dv * delta, ones) / (beta * beta)
        slopes[...] += jnp.where(cols == head, slope, 0.0)
    for r in range(nh):
        at = pl.multiple_of((me ^ r) * tl, tl)
        for u in heads:
            h = places[u][2]
            for i in range(4):
                outs[2 * r][h, i] = result[u, i, pl.ds(at, tl)].astype(BF16)
            outs[2 * r + 1][h] = result[u, 4, pl.ds(at, tl)]
        outs[2 * r + 1][hc] = slopes[pl.ds(at, tl)]


def final_terms(d, j, sc, bufs, keep, send, saved, own, came, after):
    nh, hb, tl, hc = d["nh"], d["hb"], d["tl"], d["hc"]
    part = hb // 2
    specs = []
    for _ in range(nh):
        specs.append(pl.BlockSpec((hc, 4, tl, BLOCK), lambda i, sc: (0, 0, 0, 0)))
        specs.append(pl.BlockSpec((1, tl, BLOCK), lambda i, sc: (hc, 0, 0)))
    triple = pl.BlockSpec((part, 3, BLOCK, BLOCK), lambda i, sc: (i, 0, 0, 0))
    one = pl.BlockSpec((part, BLOCK, BLOCK), lambda i, sc: (i, 0, 0))
    pair = pl.BlockSpec((part, 2, BLOCK, BLOCK), lambda i, sc: (i, 0, 0, 0))
    seven = pl.BlockSpec((2, part, 7, BLOCK, BLOCK), lambda i, sc: (0, i, 0, 0, 0))
    out_shape, out_specs = [], []
    for _ in range(nh):
        out_shape.append(struct((hc, 4, tl, BLOCK), BF16))
        out_shape.append(struct((hc + 1, tl, BLOCK)))
        out_specs.append(pl.BlockSpec((hc, 4, tl, BLOCK), lambda i, sc: (0, 0, 0, 0)))
        out_specs.append(pl.BlockSpec((hc + 1, tl, BLOCK), lambda i, sc: (0, 0, 0)))
    for _ in range(2):
        out_shape.append(struct((1, hc, BLOCK, BLOCK)))
        out_specs.append(pl.BlockSpec((1, hc, BLOCK, BLOCK), lambda i, sc: (0, 0, 0, 0)))
    return pl.pallas_call(
        functools.partial(final_kernel, d, j),
        out_shape=out_shape,
        grid_spec=pltpu.PrefetchScalarGridSpec(
            num_scalar_prefetch=1,
            grid=(hc // hb,),
            in_specs=specs + [triple, one, one, seven, pair, pair] + [ANY] * len(after),
            out_specs=out_specs,
            scratch_shapes=[
                pltpu.VMEM((hb, 4, BLOCK, BLOCK), BF16),
                pltpu.VMEM((BLOCK, BLOCK), F32),
                pltpu.VMEM((hb, 5, BLOCK, BLOCK), F32),
                pltpu.VMEM((BLOCK, BLOCK), F32),
            ],
        ),
        compiler_params=params(("arbitrary",)),
        cost_estimate=cost(7),
        name="final",
    )(sc, *bufs, keep, send[0], send[2], saved, own, came, *after)


def tokens_first(d, me, bufs, i, scratch):
    nh, hc, tl = d["nh"], d["hc"], d["tl"]
    for r in range(nh):
        rows = bufs[2 * r][:, i].astype(F32) if i < 4 else bufs[2 * r + 1][:hc]
        scratch[pl.ds((me ^ r) * hc, hc)] = rows
    return jnp.swapaxes(scratch[...], 0, 1).reshape(tl, nh, hc, BLOCK)


def early_kernel(d, sc, *refs):
    nh, tl = d["nh"], d["tl"]
    bufs, outs, scratch = refs[: 2 * nh], refs[-7:-1], refs[-1]
    for i in range(5):
        turned = tokens_first(d, sc[0], bufs, i, scratch)
        outs[i][...] = turned.reshape(outs[i].shape).astype(outs[i].dtype)
    outs[5][...] = sum(bufs[2 * r + 1][d["hc"]] for r in range(nh))


def early(d, sc, bufs, after):
    nh, hc, tl = d["nh"], d["hc"], d["tl"]
    full = (tl, nh * hc, BLOCK)
    shapes = [struct(full, BF16)] * 4 + [struct(full), struct((tl, BLOCK))]
    body = functools.partial(early_kernel, d)
    scratch = [pltpu.VMEM((nh * hc, tl, BLOCK), F32)]
    return vm_call(body, "early", shapes, sc, *bufs, after, scratch=scratch)


def unpack_kernel(d, sc, *refs):
    nh, hc, chunks, tl, heads = d["nh"], d["hc"], d["chunks"], d["tl"], d["heads"]
    before = refs[: 6 * (chunks - 1)]
    bufs, outs, scratch = refs[6 * (chunks - 1) : -7], refs[-7:-1], refs[-1]
    for i in range(5):
        parts = [
            before[6 * j + i][...].astype(F32).reshape(tl, nh, hc, BLOCK)
            for j in range(chunks - 1)
        ]
        parts.append(tokens_first(d, sc[0], bufs, i, scratch))
        whole = jnp.concatenate(parts, axis=2) if chunks > 1 else parts[0]
        outs[i][...] = whole.reshape(tl, heads, BLOCK).astype(outs[i].dtype)
    slopes = sum(bufs[2 * r + 1][hc] for r in range(nh))
    for j in range(chunks - 1):
        slopes += before[6 * j + 5][...]
    outs[5][...] = slopes[:, :heads]


def unpack(d, sc, before, bufs):
    tl, heads = d["tl"], d["heads"]
    full = (tl, heads, BLOCK)
    shapes = [struct(full, BF16)] * 4 + [struct(full), struct((tl, heads))]
    body = functools.partial(unpack_kernel, d)
    scratch = [pltpu.VMEM((d["nh"] * d["hc"], tl, BLOCK), F32)]
    return vm_call(body, "unpack", shapes, sc, *before, *bufs, [], scratch=scratch)


def exchange(d, bufs):
    nh = d["nh"]
    return [
        buf if r == 0 else lax.ppermute(buf, "head", [(i, i ^ r) for i in range(nh)])
        for r in range(nh)
        for buf in bufs[2 * r : 2 * r + 2]
    ]


def turns(chunks):
    if chunks == 2:
        return [0, 0, 1, 0, 1, 0, 1, 0, 1, 0, 1, 0, 1, 1]
    return [j for j in range(chunks) for _ in range(7)]


def per_device(d, query, key, value, decay, rate, carry_in, out_grad):
    place = lax.axis_index("seq")
    sc = jnp.stack(
        [lax.axis_index("head"), place & 1, (place >> 1) & 1, place >> 2]
    ).astype(jnp.int32)
    nh, chunks = d["nh"], d["chunks"]
    packed = pack(d, sc, query, key, value, out_grad, decay, rate)
    walks, arrivals = [], []
    for j in range(chunks):
        bufs = exchange(d, packed[2 * nh * j : 2 * nh * (j + 1)])
        walks.append(chunk_steps(d, j, sc, bufs, carry_in))
        arrivals.append(bufs[2:])
        next(walks[j])
    after, results, taken = [], {}, [0] * chunks
    for j in turns(chunks):
        early_in = arrivals[j + 1] if taken[j] == 1 and j + 1 < chunks else []
        value = walks[j].send(after + early_in)
        taken[j] += 1
        if isinstance(value, (list, tuple)):
            results[j] = value
            value = value[-1]
        after = [value]
    before, states, state_grads = [], [], []
    for j in range(chunks):
        *out, state, state_grad = results[j]
        states.append(state)
        state_grads.append(state_grad)
        back = exchange(d, out)
        if j < chunks - 1:
            before += early(d, sc, back, after)
    outs = unpack(d, sc, before, back)
    if chunks > 1:
        return (*outs, jnp.concatenate(states, axis=1), jnp.concatenate(state_grads, axis=1))
    return (*outs, states[0], state_grads[0])


def solution(mesh):
    tokens = P(("seq", "head"), None, None)
    per_block = P("seq", "head", None, None)
    table = P(("seq", "head"), None)

    def run(query, key, value, decay, rate, carry_in, out_grad):
        n, nh = mesh.shape["seq"], mesh.shape["head"]
        heads = query.shape[1]
        hg = heads // nh
        chunks = CHUNKS if hg % (4 * CHUNKS) == 0 else 1
        hc = hg // chunks
        d = {
            "n": n,
            "nh": nh,
            "heads": heads,
            "hg": hg,
            "chunks": chunks,
            "hc": hc,
            "hb": min(HB, hc),
            "tl": query.shape[0] // (n * nh),
        }
        return jax.shard_map(
            functools.partial(per_device, d),
            mesh=mesh,
            in_specs=(tokens,) * 4 + (table, P("head", None, None), tokens),
            out_specs=(tokens,) * 5 + (table, per_block, per_block),
            check_vma=False,
        )(query, key, value, decay, rate, carry_in, out_grad)

    return run
```

```python
import functools

import jax
import jax.numpy as jnp
from jax import lax
from jax.experimental import pallas as pl
from jax.experimental.pallas import tpu as pltpu
from jax.sharding import PartitionSpec as P

F32 = jnp.float32
BF16 = jnp.bfloat16
BLOCK = 128
CHUNKS = 2
ROWS = 16
PACK_BYTES = 52 * 1024 * 1024
HB = 8
FINAL_HB = 4
VMEM_BYTES = 26 * 1024 * 1024
NN = (((1,), (0,)), ((), ()))
NT = (((1,), (1,)), ((), ()))


def halves(a):
    hi = a.astype(BF16)
    return hi, (a - hi.astype(F32)).astype(BF16)


def left(a):
    hi, lo = halves(a)
    return jnp.concatenate([hi, lo], axis=1)


def dot(a, b, dims=NN):
    return lax.dot_general(a, b, dims, preferred_element_type=F32)


def mm(lhs, b):
    hi, lo = halves(b)
    row = jnp.concatenate([hi, lo], axis=1)
    both = dot(lhs, jnp.concatenate([row, row], axis=0))
    n = b.shape[1]
    return both[:, :n] + both[:, n:]


def mm_t(lhs, b):
    hi, lo = halves(b)
    rows = jnp.concatenate([hi, lo], axis=0)
    both = dot(lhs, jnp.concatenate([rows, rows], axis=1), NT)
    n = b.shape[0]
    return both[:, :n] + both[:, n:]


def mm_exact(lhs, b):
    return dot(lhs, jnp.concatenate([b, b], axis=0))


def thirds(a):
    hi = a.astype(BF16)
    rest = a - hi.astype(F32)
    mid = rest.astype(BF16)
    return hi, mid, (rest - mid.astype(F32)).astype(BF16)


def ones_product(ones, a):
    n = a.shape[1]
    parts = dot(ones, jnp.concatenate(thirds(a), axis=1))
    return parts[:, :n] + parts[:, n : 2 * n] + parts[:, 2 * n :]


def rows_cols():
    shape = (BLOCK, BLOCK)
    return lax.broadcasted_iota(jnp.int32, shape, 0), lax.broadcasted_iota(jnp.int32, shape, 1)


def unit_rate(x):
    return lax.rsqrt(jnp.sum(x * x, axis=-1, keepdims=True) + 1e-06)


def params(kind=None):
    return pltpu.CompilerParams(vmem_limit_bytes=VMEM_BYTES, dimension_semantics=kind)


def struct(shape, dtype=F32):
    return jax.ShapeDtypeStruct(shape, dtype)


SMEM = pl.BlockSpec(memory_space=pltpu.SMEM)


def cost(micros):
    return pl.CostEstimate(flops=int(micros * 1e10), bytes_accessed=0, transcendentals=0)


def pack_kernel(d, sc, q, k, v, g, decay, rate, *outs_scratch):
    outs, scratch = outs_scratch[:-1], outs_scratch[-1]
    me = sc[0]
    nh, hg, hc, chunks, heads = d["nh"], d["hg"], d["hc"], d["chunks"], d["heads"]
    for i, ref in enumerate((q, k, v, g, decay)):
        scratch[...] = jnp.swapaxes(ref[...].astype(F32), 0, 1)
        for j in range(chunks):
            for r in range(nh):
                bout, fout = outs[2 * (j * nh + r)], outs[2 * (j * nh + r) + 1]
                rows = scratch[pl.ds((me ^ r) * hg + j * hc, hc)]
                if i < 4:
                    bout[:, i] = rows.astype(BF16)
                else:
                    fout[:hc] = rows
    wide = jnp.concatenate([rate[...], jnp.zeros((ROWS, BLOCK - heads), F32)], axis=1)
    for j in range(chunks):
        for r in range(nh):
            outs[2 * (j * nh + r) + 1][hc] = wide


def pack(d, sc, q, k, v, g, decay, rate):
    hc, tl, heads = d["hc"], d["tl"], d["heads"]
    shapes, specs = [], []
    for _ in range(d["chunks"] * d["nh"]):
        shapes.append(struct((hc, 4, tl, BLOCK), BF16))
        shapes.append(struct((hc + 1, tl, BLOCK)))
        specs.append(pl.BlockSpec((hc, 4, ROWS, BLOCK), lambda i: (0, 0, i, 0)))
        specs.append(pl.BlockSpec((hc + 1, ROWS, BLOCK), lambda i: (0, i, 0)))
    block = pl.BlockSpec((ROWS, heads, BLOCK), lambda i: (i, 0, 0))
    return pl.pallas_call(
        functools.partial(pack_kernel, d),
        out_shape=shapes,
        grid=(tl // ROWS,),
        in_specs=[SMEM] + [block] * 5 + [pl.BlockSpec((ROWS, heads), lambda i: (i, 0))],
        out_specs=specs,
        scratch_shapes=[pltpu.VMEM((heads, ROWS, BLOCK), F32)],
        compiler_params=pltpu.CompilerParams(
            vmem_limit_bytes=PACK_BYTES, dimension_semantics=("arbitrary",)
        ),
        cost_estimate=cost(4),
        name="pack",
    )(sc, q, k, v, g, decay, rate)


def order(d, sc, step):
    part = d["hb"] // 2
    places = []
    for u in range(d["hb"]):
        half, i = u // part, step * part + u % part
        places.append((half, u % part, (half ^ sc[1]) * (d["hc"] // 2) + i))
    return places


def gather_rows(d, me, bufs, places, halves_ref, wide_ref, table, last):
    tl = d["tl"]
    for r in range(d["nh"]):
        at = pl.multiple_of((me ^ r) * tl, tl)
        for u, (_, _, h) in enumerate(places):
            for i in range(4):
                halves_ref[u, i, pl.ds(at, tl)] = bufs[2 * r][h, i]
            if wide_ref is not None:
                wide_ref[u, pl.ds(at, tl)] = bufs[2 * r + 1][h]
        table[pl.ds(at, tl)] = bufs[2 * r + 1][last]


def spread_rate(table, head):
    rows = lax.broadcasted_iota(jnp.int32, (3 * BLOCK, BLOCK), 0)
    pick = jnp.where((rows & (BLOCK - 1)) == head, 1.0, 0.0).astype(BF16)
    return dot(table, pick)


def lane_sums(x, ones):
    return mm_exact(left(x), ones)


def local_kernel(d, j, sc, *refs):
    nh, hb, hg, hc = d["nh"], d["hb"], d["hg"], d["hc"]
    bufs = refs[: 2 * nh]
    keep, send, saved = refs[-10], refs[-9:-6], refs[-6]
    thin, wide_rows, rates, below, inverse = refs[-5:]
    me = sc[0]
    places = order(d, sc, pl.program_id(0))
    gather_rows(d, me, bufs, places, thin, wide_rows, rates, hc)
    rows, cols = rows_cols()
    tri = jnp.where(rows >= cols, 1.0, 0.0).astype(BF16)
    ones = jnp.ones((BLOCK, BLOCK), BF16)
    apart = rows ^ cols
    table = jnp.concatenate(thirds(rates[...]), axis=1)
    heads = range(hb)
    lower, cross, crosst, kpos, kend, qpos, fade, beta = [], [], [], [], [], [], [], []
    for u in heads:
        half, i, h = places[u]
        q, k, decay = thin[u, 0].astype(F32), thin[u, 1].astype(F32), wide_rows[u]
        qn = q * lax.rsqrt(lane_sums(q * q, ones) + 1e-06)
        kn = k * lax.rsqrt(lane_sums(k * k, ones) + 1e-06)
        cum = ones_product(tri, decay)
        mid = 0.5 * cum[BLOCK - 1 :]
        grow = jnp.exp(cum - mid)
        shrink = jnp.exp(mid - cum)
        em = jnp.exp(mid)
        kc, kneg, qc = kn * grow, kn * shrink, qn * grow
        both = mm_t(left(jnp.concatenate([kc, qc], axis=0)), kneg)
        beta.append(spread_rate(table, me * hg + j * hc + h))
        lower.append(jnp.where(rows > cols, both[:BLOCK], 0.0) * beta[u])
        cross.append(jnp.where(rows >= cols, both[BLOCK:], 0.0))
        crosst.append(jnp.where(rows <= cols, mm_t(left(kneg), qc), 0.0))
        kpos.append(kc * em)
        qpos.append(qc * em)
        kend.append(kneg * em)
        fade.append(jnp.where(rows == cols, em * em, 0.0))
        saved[half, i, 6] = cum
    for u in heads:
        below[u] = lower[u]
        inverse[u] = jnp.where(rows == cols, 1.0, jnp.where(apart == 1, -lower[u], 0.0))

    def double(level, _):
        off = (apart >> level) == 1
        mids = [mm(left(jnp.where(off, below[u], 0.0)), inverse[u]) for u in heads]
        for u in heads:
            inverse[u] -= mm(left(inverse[u]), mids[u])
        return 0

    for level in range(1, BLOCK.bit_length() - 1):
        double(level, 0)
    for u in heads:
        half, i, _ = places[u]
        v, g = thin[u, 2].astype(F32), thin[u, 3]
        scaled = jnp.concatenate([beta[u] * kpos[u], beta[u] * v], axis=1)
        solved = mm(left(inverse[u]), scaled)
        by = mm(left(jnp.concatenate([cross[u], kend[u].T], axis=0)), solved)
        reach = qpos[u] - by[:BLOCK, :BLOCK]
        hi, lo = halves(reach)
        feed = dot(g.T, jnp.concatenate([hi, lo], axis=1))
        own = (fade[u] - by[BLOCK:, :BLOCK], by[BLOCK:, BLOCK:], feed[:, :BLOCK] + feed[:, BLOCK:])
        for t in range(3):
            if half:
                send[t][i] = own[t]
            else:
                keep[i, t] = own[t]
        saved[half, i, 0] = solved[:, :BLOCK]
        saved[half, i, 1] = solved[:, BLOCK:]
        saved[half, i, 2] = reach
        saved[half, i, 3] = by[:BLOCK, BLOCK:]
        seen = mm_exact(left(crosst[u]), g)
        back = mm(left(inverse[u].T), jnp.concatenate([kend[u], seen], axis=1))
        saved[half, i, 4] = beta[u] * back[:, :BLOCK]
        saved[half, i, 5] = beta[u] * back[:, BLOCK:]


ANY = pl.BlockSpec(memory_space=pl.ANY)


def local_terms(d, j, sc, bufs, after):
    nh, hb, tl, hc = d["nh"], d["hb"], d["tl"], d["hc"]
    part = hb // 2
    specs = []
    for _ in range(nh):
        specs.append(pl.BlockSpec((hc, 4, tl, BLOCK), lambda i, sc: (0, 0, 0, 0)))
        specs.append(pl.BlockSpec((hc + 1, tl, BLOCK), lambda i, sc: (0, 0, 0)))
    triple = pl.BlockSpec((part, 3, BLOCK, BLOCK), lambda i, sc: (i, 0, 0, 0))
    return pl.pallas_call(
        functools.partial(local_kernel, d, j),
        out_shape=[
            struct((hc // 2, 3, BLOCK, BLOCK)),
            *[struct((hc // 2, BLOCK, BLOCK))] * 3,
            struct((2, hc // 2, 7, BLOCK, BLOCK)),
        ],
        grid_spec=pltpu.PrefetchScalarGridSpec(
            num_scalar_prefetch=1,
            grid=(hc // hb,),
            in_specs=specs + [ANY] * len(after),
            out_specs=[
                triple,
                *[pl.BlockSpec((part, BLOCK, BLOCK), lambda i, sc: (i, 0, 0))] * 3,
                pl.BlockSpec((2, part, 7, BLOCK, BLOCK), lambda i, sc: (0, i, 0, 0, 0)),
            ],
            scratch_shapes=[
                pltpu.VMEM((hb, 4, BLOCK, BLOCK), BF16),
                pltpu.VMEM((hb, BLOCK, BLOCK), F32),
                pltpu.VMEM((BLOCK, BLOCK), F32),
                pltpu.VMEM((hb, BLOCK, BLOCK), F32),
                pltpu.VMEM((hb, BLOCK, BLOCK), F32),
            ],
        ),
        compiler_params=params(("arbitrary",)),
        cost_estimate=cost(10),
        name="local",
    )(sc, *bufs, *after)


def term(maps, h, i):
    return maps[i][h] if isinstance(maps, tuple) else maps[h, i]


def forward_state(maps, h, state):
    return mm(left(term(maps, h, 0)), state) + term(maps, h, 1)


def backward_state(maps, h, grad):
    return mm(left(grad), term(maps, h, 0)) + term(maps, h, 2)


def join_maps(a, b, h, ref, i):
    by = mm(left(jnp.concatenate([term(b, h, 0), term(b, h, 2)], axis=0)), term(a, h, 0))
    ref[i, 0] = by[:BLOCK]
    ref[i, 1] = mm(left(term(b, h, 0)), term(a, h, 1)) + term(b, h, 1)
    ref[i, 2] = by[BLOCK:] + term(a, h, 2)


def join_kernel(n, sc, mine, *refs):
    other, (keep, send) = tuple(refs[:3]), refs[3:]

    def run(a, b):
        for i in range(n):
            for ref, s in ((keep, sc[2]), (send, 1 - sc[2])):
                join_maps(a, b, s * n + i, ref, i)

    @pl.when(sc[1] == 0)
    def _():
        run(mine, other)

    @pl.when(sc[1] == 1)
    def _():
        run(other, mine)


def vm_call(body, name, out_shape, *args, scratch=()):
    vm = pl.BlockSpec(memory_space=pltpu.VMEM)
    many = isinstance(out_shape, list)
    reads, waits = len(args) - 1, len(args[-1])

    def skip(*refs):
        body(*refs[:reads], *refs[reads + waits :])

    return pl.pallas_call(
        skip,
        out_shape=out_shape,
        in_specs=[SMEM] + [vm] * (len(args) - 2) + [ANY] * len(args[-1]),
        out_specs=[vm] * len(out_shape) if many else vm,
        scratch_shapes=list(scratch),
        compiler_params=params(),
        cost_estimate=cost(0 if name in ("join", "core") else 1),
        name=name,
    )(*args[:-1], *args[-1])


def carry_base(j, hc, sc):
    return j * hc + sc[1] * (hc // 2) + sc[2] * (hc // 4)


def plane_kernel(j, hc, sc, mine, other, carry, plane, pay):
    n = hc // 4
    base = carry_base(j, hc, sc)

    def run(a, b):
        for h in range(n):
            join_maps(a, b, h, plane, h)

    @pl.when(sc[2] == 0)
    def _():
        run(mine, other)

    @pl.when(sc[2] == 1)
    def _():
        run(other, mine)

    pay[:, 1] = plane[:, 0]

    @pl.when(sc[3] == 0)
    def _():
        for h in range(n):
            pay[h, 0] = forward_state(plane, h, carry[base + h])

    @pl.when((sc[3] != 0) & (sc[3] & 1 == 0))
    def _():
        pay[:, 0] = plane[:, 1]

    @pl.when(sc[3] & 1 == 1)
    def _():
        pay[:, 0] = plane[:, 2]


def middle_kernel(n, sc, plane, got, turn):
    @pl.when(sc[3] == 1)
    def _():
        for h in range(n):
            turn[h] = forward_state(plane, h, got[h, 0])

    @pl.when(sc[3] == 2)
    def _():
        for h in range(n):
            turn[h] = backward_state(plane, h, got[h, 0])

    @pl.when((sc[3] == 0) | (sc[3] == 3))
    def _():
        turn[...] = jnp.zeros_like(turn)


def spread_x(n, sc, state, grad, mine, other, keep, send):
    @pl.when(sc[2] == 0)
    def _():
        for h in range(n):
            keep[h, 0] = state[h]
            keep[h, 1] = backward_state(other, h, grad[h])
            send[h, 0] = forward_state(mine, h, state[h])
            send[h, 1] = grad[h]

    @pl.when(sc[2] == 1)
    def _():
        for h in range(n):
            keep[h, 0] = forward_state(other, h, state[h])
            keep[h, 1] = grad[h]
            send[h, 0] = state[h]
            send[h, 1] = backward_state(mine, h, grad[h])


def last_kernel(j, hc, sc, carry, got, near, far, mine, other, keep, send, state, grad):
    n = hc // 4
    base = carry_base(j, hc, sc)

    @pl.when(sc[3] == 0)
    def _():
        for h in range(n):
            state[h] = carry[base + h]
            grad[h] = mm(left(far[h]), got[h, 1]) + got[h, 0]

    @pl.when(sc[3] == 1)
    def _():
        state[...] = got[:, 0]
        grad[...] = near[...]

    @pl.when(sc[3] == 2)
    def _():
        state[...] = near[...]
        grad[...] = got[:, 0]

    @pl.when(sc[3] == 3)
    def _():
        for h in range(n):
            state[h] = mm(left(got[h, 1]), far[h]) + got[h, 0]
        grad[...] = jnp.zeros_like(grad)

    spread_x(n, sc, state, grad, mine, other, keep, send)


def hop_kernel(j, hc, groups, sc, plane, carry, up, down, ahead, behind):
    base = carry_base(j, hc, sc)
    for h in range(hc // 4):
        entering = jnp.where(sc[3] == 0, carry[base + h], up[h])
        leaving = jnp.where(sc[3] == groups - 1, 0.0, down[h])
        ahead[h] = forward_state(plane, h, entering)
        behind[h] = backward_state(plane, h, leaving)


def end_kernel(j, hc, groups, sc, carry, up, down, mine, other, keep, send, state, grad):
    n = hc // 4
    base = carry_base(j, hc, sc)
    for h in range(n):
        state[h] = jnp.where(sc[3] == 0, carry[base + h], up[h])
        grad[h] = jnp.where(sc[3] == groups - 1, 0.0, down[h])
    spread_x(n, sc, state, grad, mine, other, keep, send)


def core_kernel(n, sc, own, came, mine, *refs):
    other, keep, send = tuple(refs[:3]), refs[3], refs[4:]

    def run(first):
        for half, source in ((sc[2], own), (1 - sc[2], came)):
            for i in range(n):
                h = half * n + i
                state, grad = source[i, 0], source[i, 1]
                if first:
                    keep[h, 0] = state
                    keep[h, 1] = backward_state(other, h, grad)
                    send[0][h] = forward_state(mine, h, state)
                    send[1][h] = grad
                else:
                    keep[h, 0] = forward_state(other, h, state)
                    keep[h, 1] = grad
                    send[0][h] = state
                    send[1][h] = backward_state(mine, h, grad)

    @pl.when(sc[1] == 0)
    def _():
        run(True)

    @pl.when(sc[1] == 1)
    def _():
        run(False)


def swap(array, n, stride):
    return lax.ppermute(array, "seq", [(i, i ^ stride) for i in range(n)])


def move(array, pairs):
    return lax.ppermute(array, "seq", [(4 * a + k, 4 * b + k) for a, b in pairs for k in range(4)])


def chunk_steps(d, j, sc, bufs, carry):
    n, hc, groups = d["n"], d["hc"], d["n"] // 4
    half, quarter = hc // 2, hc // 4
    single = struct((quarter, BLOCK, BLOCK))
    pair = struct((quarter, 2, BLOCK, BLOCK))
    pair_c = struct((half, 2, BLOCK, BLOCK))
    single_c = struct((half, BLOCK, BLOCK))
    triple = struct((quarter, 3, BLOCK, BLOCK))
    scratch = [pltpu.VMEM((quarter, BLOCK, BLOCK), F32)] * 2
    after = yield
    keep, *send, saved = local_terms(d, j, sc, bufs, after)
    after = yield keep
    came = [swap(part, n, 1) for part in send]
    body = functools.partial(join_kernel, quarter)
    keep_x, send_x = vm_call(body, "join", [triple, triple], sc, keep, *came, after)
    after = yield send_x
    came_x = swap(send_x, n, 2)
    body = functools.partial(plane_kernel, j, hc)
    plane, pay = vm_call(body, "plane", [triple, pair], sc, keep_x, came_x, carry, after)
    after = yield pay
    if groups == 4:
        got = move(pay, [(0, 1), (1, 0), (2, 3), (3, 2)])
        body = functools.partial(middle_kernel, quarter)
        turn = vm_call(body, "middle", single, sc, plane, got, after)
        after = yield turn
        near = move(turn, [(1, 2), (2, 1)])
        far = move(turn, [(1, 3), (2, 0)])
        body = functools.partial(last_kernel, j, hc)
        args = (sc, carry, got, near, far, keep_x, came_x, after)
        own_x, give_x = vm_call(body, "spread", [pair, pair], *args, scratch=scratch)
    else:
        up_in = jnp.zeros((quarter, BLOCK, BLOCK), F32)
        down_in = up_in
        upward = [(i, i + 1) for i in range(groups - 1)]
        downward = [(i + 1, i) for i in range(groups - 1)]
        body = functools.partial(hop_kernel, j, hc, groups)

        def hop(_, at):
            ahead, behind = vm_call(body, "hop", [single, single], sc, plane, carry, *at, [])
            return move(ahead, upward), move(behind, downward)

        up_in, down_in = lax.fori_loop(0, groups - 1, hop, (up_in, down_in))
        after = yield up_in
        body = functools.partial(end_kernel, j, hc, groups)
        args = (sc, carry, up_in, down_in, keep_x, came_x, after)
        own_x, give_x = vm_call(body, "spread", [pair, pair], *args, scratch=scratch)
    after = yield give_x
    got_x = swap(give_x, n, 2)
    body = functools.partial(core_kernel, quarter)
    out_shape = [pair_c, single_c, single_c]
    own, *give = vm_call(body, "core", out_shape, sc, own_x, got_x, keep, *came, after)
    after = yield own
    arrived = [swap(part, n, 1) for part in give]
    outs = final_terms(d, j, sc, bufs, keep, send, saved, own, arrived, after)
    yield outs


def final_kernel(d, j, sc, *refs):
    nh, hb, tl, hg, hc = d["nh"], d["hb"], d["tl"], d["hg"], d["hc"]
    bufs, refs = refs[: 2 * nh], refs[2 * nh :]
    keep, send, (saved, own), came = refs[0], refs[1:3], refs[3:5], refs[5:7]
    outs = refs[-6 - 2 * nh : -6]
    states, state_grads, thin, rates, result, slopes = refs[-6:]
    step = pl.program_id(0)
    me = sc[0]
    places = order(d, sc, step)
    gather_rows(d, me, bufs, places, thin, None, rates, 0)
    rows, cols = rows_cols()
    upper = jnp.where(rows <= cols, 1.0, 0.0).astype(BF16)
    ones = jnp.ones((BLOCK, BLOCK), BF16)
    table = jnp.concatenate(thirds(rates[...]), axis=1)
    heads = range(hb)

    @pl.when(step == 0)
    def _():
        slopes[...] = jnp.zeros_like(slopes)

    for u in heads:
        half, i, h = places[u]
        transit = send[0][i] if half else keep[i, 0]
        feed = send[1][i] if half else keep[i, 2]
        q, k, g = thin[u, 0].astype(F32), thin[u, 1].astype(F32), thin[u, 3].astype(F32)
        rq = lax.rsqrt(lane_sums(q * q, ones) + 1e-06)
        rk = lax.rsqrt(lane_sums(k * k, ones) + 1e-06)
        qn, kn = q * rq, k * rk
        cum = saved[half, i, 6]
        mid = 0.5 * cum[BLOCK - 1 :]
        grow, shrink, em = jnp.exp(cum - mid), jnp.exp(mid - cum), jnp.exp(mid)
        kc, kneg, qc = kn * grow, kn * shrink, qn * grow
        state, grad = (came[0][i], came[1][i]) if half else (own[i, 0], own[i, 1])
        known = mm(left(jnp.concatenate([saved[half, i, 0], saved[half, i, 2]], axis=0)), state)
        delta = saved[half, i, 1] - known[:BLOCK]
        result[u, 0] = saved[half, i, 3] + known[BLOCK:]
        dv = saved[half, i, 5] + mm_t(left(saved[half, i, 4]), grad)
        result[u, 3] = dv
        states[0, h] = state
        wide_d, wide_s = left(delta), left(state)
        by_grad = mm(jnp.concatenate([wide_d, wide_s], axis=0), grad)
        tail = em * by_grad[:BLOCK]
        mixed = jnp.sum(jnp.where(rows == cols, by_grad[BLOCK:], 0.0), axis=0, keepdims=True)
        state_grads[0, h] = (feed + mm(left(grad), transit)).T
        both = jnp.concatenate([g, -dv], axis=0)
        gd = left(both)
        weights = mm_t(gd, delta)
        flipped = mm_t(wide_d, both)
        cross = jnp.where(rows >= cols, weights[:BLOCK], 0.0)
        inner = jnp.where(rows > cols, weights[BLOCK:], 0.0)
        crosst = jnp.where(rows <= cols, flipped[:, :BLOCK], 0.0)
        innert = jnp.where(rows < cols, flipped[:, BLOCK:], 0.0)
        pos = mm(left(jnp.concatenate([cross, inner], axis=0)), kneg) + em * mm_t(gd, state)
        dqc, dkc = pos[:BLOCK], pos[BLOCK:]
        dkneg = tail + mm(
            left(jnp.concatenate([crosst, innert], axis=1)), jnp.concatenate([qc, kc], axis=0)
        )
        dqn = dqc * grow
        dkn = dkc * grow + dkneg * shrink
        result[u, 1] = rq * (dqn - qn * lane_sums(qn * dqn, ones))
        result[u, 2] = rk * (dkn - kn * lane_sums(kn * dkn, ones))
        dcum = qc * dqc + kc * dkc - kneg * dkneg
        end = jnp.sum(kneg * tail, axis=0, keepdims=True) + em * em * mixed
        result[u, 4] = ones_product(upper, dcum) + end
        head = me * hg + j * hc + h
        beta = spread_rate(table, head)
        slope = lane_sums(dv * delta, ones) / (beta * beta)
        slopes[...] += jnp.where(cols == head, slope, 0.0)
    for r in range(nh):
        at = pl.multiple_of((me ^ r) * tl, tl)
        for u in heads:
            h = places[u][2]
            for i in range(4):
                outs[2 * r][h, i] = result[u, i, pl.ds(at, tl)].astype(BF16)
            outs[2 * r + 1][h] = result[u, 4, pl.ds(at, tl)]
        outs[2 * r + 1][hc] = slopes[pl.ds(at, tl)]


def final_terms(d, j, sc, bufs, keep, send, saved, own, came, after):
    d = dict(d, hb=min(FINAL_HB, d["hb"]))
    nh, hb, tl, hc = d["nh"], d["hb"], d["tl"], d["hc"]
    part = hb // 2
    specs = []
    for _ in range(nh):
        specs.append(pl.BlockSpec((hc, 4, tl, BLOCK), lambda i, sc: (0, 0, 0, 0)))
        specs.append(pl.BlockSpec((1, tl, BLOCK), lambda i, sc: (hc, 0, 0)))
    triple = pl.BlockSpec((part, 3, BLOCK, BLOCK), lambda i, sc: (i, 0, 0, 0))
    one = pl.BlockSpec((part, BLOCK, BLOCK), lambda i, sc: (i, 0, 0))
    pair = pl.BlockSpec((part, 2, BLOCK, BLOCK), lambda i, sc: (i, 0, 0, 0))
    seven = pl.BlockSpec((2, part, 7, BLOCK, BLOCK), lambda i, sc: (0, i, 0, 0, 0))
    out_shape, out_specs = [], []
    for _ in range(nh):
        out_shape.append(struct((hc, 4, tl, BLOCK), BF16))
        out_shape.append(struct((hc + 1, tl, BLOCK)))
        out_specs.append(pl.BlockSpec((hc, 4, tl, BLOCK), lambda i, sc: (0, 0, 0, 0)))
        out_specs.append(pl.BlockSpec((hc + 1, tl, BLOCK), lambda i, sc: (0, 0, 0)))
    for _ in range(2):
        out_shape.append(struct((1, hc, BLOCK, BLOCK)))
        out_specs.append(pl.BlockSpec((1, hc, BLOCK, BLOCK), lambda i, sc: (0, 0, 0, 0)))
    return pl.pallas_call(
        functools.partial(final_kernel, d, j),
        out_shape=out_shape,
        grid_spec=pltpu.PrefetchScalarGridSpec(
            num_scalar_prefetch=1,
            grid=(hc // hb,),
            in_specs=specs + [triple, one, one, seven, pair, one, one] + [ANY] * len(after),
            out_specs=out_specs,
            scratch_shapes=[
                pltpu.VMEM((hb, 4, BLOCK, BLOCK), BF16),
                pltpu.VMEM((BLOCK, BLOCK), F32),
                pltpu.VMEM((hb, 5, BLOCK, BLOCK), F32),
                pltpu.VMEM((BLOCK, BLOCK), F32),
            ],
        ),
        compiler_params=params(("arbitrary",)),
        cost_estimate=cost(0),
        name="final",
    )(sc, *bufs, keep, send[0], send[2], saved, own, *came, *after)


def tokens_first(d, me, bufs, i, scratch):
    nh, hc = d["nh"], d["hc"]
    for r in range(nh):
        rows = bufs[2 * r][:, i].astype(F32) if i < 4 else bufs[2 * r + 1][:hc]
        scratch[pl.ds((me ^ r) * hc, hc)] = rows
    return jnp.swapaxes(scratch[...], 0, 1).reshape(ROWS, nh, hc, BLOCK)


def early_kernel(d, sc, *refs):
    nh = d["nh"]
    bufs, outs, scratch = refs[: 2 * nh], refs[-7:-1], refs[-1]
    for i in range(5):
        turned = tokens_first(d, sc[0], bufs, i, scratch)
        outs[i][...] = turned.reshape(outs[i].shape).astype(outs[i].dtype)
    outs[5][...] = sum(bufs[2 * r + 1][d["hc"]] for r in range(nh))


def unpack_kernel(d, sc, *refs):
    nh, hc, chunks, heads = d["nh"], d["hc"], d["chunks"], d["heads"]
    before = refs[: 6 * (chunks - 1)]
    bufs, outs, scratch = refs[6 * (chunks - 1) : -7], refs[-7:-1], refs[-1]
    for i in range(5):
        parts = [
            before[6 * j + i][...].astype(F32).reshape(ROWS, nh, hc, BLOCK)
            for j in range(chunks - 1)
        ]
        parts.append(tokens_first(d, sc[0], bufs, i, scratch))
        whole = jnp.concatenate(parts, axis=2) if chunks > 1 else parts[0]
        outs[i][...] = whole.reshape(ROWS, heads, BLOCK).astype(outs[i].dtype)
    slopes = sum(bufs[2 * r + 1][hc] for r in range(nh))
    for j in range(chunks - 1):
        slopes += before[6 * j + 5][...]
    outs[5][...] = slopes[:, :heads]


def by_tokens(d, body, name, heads, width, sc, before, bufs, after):
    nh, hc, tl = d["nh"], d["hc"], d["tl"]
    reads, waits = 1 + len(before) + len(bufs), len(after)

    def skip(*refs):
        body(d, *refs[:reads], *refs[reads + waits :])

    three = lambda n: pl.BlockSpec((ROWS, n, BLOCK), lambda i: (i, 0, 0))
    two = lambda n: pl.BlockSpec((ROWS, n), lambda i: (i, 0))
    old = ([three(nh * hc)] * 5 + [two(BLOCK)]) * (len(before) // 6)
    new = [
        pl.BlockSpec((hc, 4, ROWS, BLOCK), lambda i: (0, 0, i, 0)),
        pl.BlockSpec((hc + 1, ROWS, BLOCK), lambda i: (0, i, 0)),
    ] * nh
    full = (tl, heads, BLOCK)
    return pl.pallas_call(
        skip,
        out_shape=[struct(full, BF16)] * 4 + [struct(full), struct((tl, width))],
        grid=(tl // ROWS,),
        in_specs=[SMEM] + old + new + [ANY] * waits,
        out_specs=[three(heads)] * 5 + [two(width)],
        scratch_shapes=[pltpu.VMEM((nh * hc, ROWS, BLOCK), F32)],
        compiler_params=params(("arbitrary",)),
        cost_estimate=cost(2),
        name=name,
    )(sc, *before, *bufs, *after)


def exchange(d, bufs):
    nh = d["nh"]
    return [
        buf if r == 0 else lax.ppermute(buf, "head", [(i, i ^ r) for i in range(nh)])
        for r in range(nh)
        for buf in bufs[2 * r : 2 * r + 2]
    ]


def turns(chunks):
    if chunks == 2:
        return [0, 0, 1, 0, 1, 0, 1, 0, 1, 0, 0, 1, 1, 1]
    return [j for j in range(chunks) for _ in range(7)]


def per_device(d, query, key, value, decay, rate, carry_in, out_grad):
    place = lax.axis_index("seq")
    sc = jnp.stack(
        [lax.axis_index("head"), place & 1, (place >> 1) & 1, place >> 2]
    ).astype(jnp.int32)
    nh, chunks = d["nh"], d["chunks"]
    packed = pack(d, sc, query, key, value, out_grad, decay, rate)
    walks, arrivals = [], []
    for j in range(chunks):
        bufs = exchange(d, packed[2 * nh * j : 2 * nh * (j + 1)])
        walks.append(chunk_steps(d, j, sc, bufs, carry_in))
        arrivals.append(bufs[2:])
        next(walks[j])
    after, results, taken = [], {}, [0] * chunks
    for j in turns(chunks):
        early_in = []
        value = walks[j].send(after + early_in)
        taken[j] += 1
        if isinstance(value, (list, tuple)):
            results[j] = value
            value = value[-1]
        after = [value]
    before, states, state_grads = [], [], []
    for j in range(chunks):
        *out, state, state_grad = results[j]
        states.append(state)
        state_grads.append(state_grad)
        back = exchange(d, out)
        if j < chunks - 1:
            before += by_tokens(
                d, early_kernel, "early", nh * d["hc"], BLOCK, sc, [], back, after
            )
    outs = by_tokens(
        d, unpack_kernel, "unpack", d["heads"], d["heads"], sc, before, back, []
    )
    if chunks > 1:
        return (*outs, jnp.concatenate(states, axis=1), jnp.concatenate(state_grads, axis=1))
    return (*outs, states[0], state_grads[0])


def solution(mesh):
    tokens = P(("seq", "head"), None, None)
    per_block = P("seq", "head", None, None)
    table = P(("seq", "head"), None)

    def run(query, key, value, decay, rate, carry_in, out_grad):
        n, nh = mesh.shape["seq"], mesh.shape["head"]
        heads = query.shape[1]
        hg = heads // nh
        chunks = CHUNKS if hg % (4 * CHUNKS) == 0 else 1
        hc = hg // chunks
        d = {
            "n": n,
            "nh": nh,
            "heads": heads,
            "hg": hg,
            "chunks": chunks,
            "hc": hc,
            "hb": min(HB, hc),
            "tl": query.shape[0] // (n * nh),
        }
        return jax.shard_map(
            functools.partial(per_device, d),
            mesh=mesh,
            in_specs=(tokens,) * 4 + (table, P("head", None, None), tokens),
            out_specs=(tokens,) * 5 + (table, per_block, per_block),
            check_vma=False,
        )(query, key, value, decay, rate, carry_in, out_grad)

    return run
```
